32 devices in a mesh: ctx: 4 (over z), fsdp: 8 (over y, x, core).
Axes of the slice: x: 2, y: 2, z: 4, core: 2. Of those that a mesh axis runs over, the one named last changes fastest.
Arguments:
- hidden: bfloat16 [8, 1024, 1024], P('fsdp', 'ctx'), may hold values from -6 to 6
- cotangent: bfloat16 [8, 1024, 1024], P('fsdp', 'ctx'), may hold values from -6 to 6
- doc_ids: int32 [8, 1024], P('fsdp', 'ctx'), may hold values from 0 to 2, as said below
- mixer_in_weight: bfloat16 [1024, 4120], P('fsdp'), may hold values from -0.1875 to 0.1875
- mixer_out_weight: bfloat16 [2048, 1024], P('fsdp'), may hold values from -0.375 to 0.375
- feedforward_in_weight: bfloat16 [1024, 4096], P('fsdp'), may hold values from -0.1875 to 0.1875
- feedforward_out_weight: bfloat16 [2048, 1024], P('fsdp'), may hold values from -0.125 to 0.125
- gain_in: bfloat16 [1024], P('fsdp'), may hold values from 0.5 to 1.5
- gain_ff: bfloat16 [1024], P('fsdp'), may hold values from 0.5 to 1.5
- gain_mix: bfloat16 [1536], P('fsdp'), may hold values from 0.5 to 1.5
- conv_weight: bfloat16 [1792, 4], P('fsdp'), may hold values from -3 to 3
- conv_bias: bfloat16 [1792], P('fsdp'), may hold values from -0.5 to 0.5
- dt_bias: float32 [24], replicated, may hold values from -3 to -1
- a_log: float32 [24], replicated, may hold values from -8 to 1
- d_skip: float32 [24], replicated, may hold values from 0.5 to 1.5
Outputs:
- output: bfloat16 [8, 1024, 1024], P('fsdp', 'ctx')
- grad_hidden: float32 [8, 1024, 1024], P('fsdp', 'ctx')
- grad_w_mix_in: float32 [1024, 4120], P('fsdp')
- grad_w_mix_out: float32 [2048, 1024], P('fsdp')
- grad_w_ffn_in: float32 [1024, 4096], P('fsdp')
- grad_w_ffn_out: float32 [2048, 1024], P('fsdp')
- grad_gain_in: float32 [1024], P('fsdp')
- grad_gain_ff: float32 [1024], P('fsdp')
- grad_gain_mix: float32 [1536], P('fsdp')
- grad_conv_weight: float32 [1792, 4], P('fsdp')
- grad_conv_bias: float32 [1792], P('fsdp')
- grad_dt_bias: float32 [24], replicated
- grad_a_log: float32 [24], replicated
- grad_d_skip: float32 [24], replicated
The draws below stay inside these ranges and needn't reach their ends.
Inputs may be any that keep to these rules, and one draw needn't show every extreme that they name: `doc_ids`: each row's ids never fall, start at 0 and take each of 0, 1 and 2.
All inputs are finite; a program needn't handle non-finite values.
Results may differ from the reference program's by a relative error of at most 0.017.
Values may be sent and summed in bfloat16 or wider, within the bound.
No kernel may reach another device: no remote copies, remote signals or barrier semaphores. Data moves between devices by JAX's collectives and lax.ppermute only.
A program may use at most 256 MiB of HBM per device.

```python
import math
import jax
import jax.numpy as jnp
from jax import lax

D = 1024
FF = 2048
NHQ = 8
NHKV = 2
HD = 64
MH = 24
MP = 64
NSTATE = 128
CONVK = 4
STRETCH = 128
LEN = 1024
TOK_DEV = 256
SEQS = 8
GQ = 4
ATTW = 512
KVW = 128
MDIM = 1536
CONVC = 1792
MIXW = 2048
NIN = 4120


def draw_doc_ids(key, part):
    key = jax.random.fold_in(key, 7)
    order_key, first_key, second_key, near_key, far_key = jax.random.split(key, 5)
    spanning = (jax.random.permutation(order_key, SEQS) < (SEQS + 1) // 2)[:, None]
    first_free = jax.random.randint(first_key, (SEQS, 1), 1, LEN // 2)
    second_free = jax.random.randint(second_key, (SEQS, 1), first_free + 1, LEN)
    first_near = jax.random.randint(near_key, (SEQS, 1), 1, TOK_DEV)
    second_far = jax.random.randint(far_key, (SEQS, 1), LEN - TOK_DEV + 1, LEN)
    first_end = jnp.where(spanning, first_near, first_free)
    second_start = jnp.where(spanning, second_far, second_free)
    places = jnp.arange(LEN, dtype=jnp.int32)[None, :]
    return (places >= first_end).astype(jnp.int32) + (places >= second_start).astype(jnp.int32)


def level_of(rng, extent, cuts, smallest, top_value):
    def one(position, shards_of):
        draws = jax.random.uniform(jax.random.fold_in(jax.random.fold_in(rng, 6), position), (shards_of,), jnp.float32, smallest / len(cuts), top_value / len(cuts))
        return jnp.repeat(jnp.exp(draws), extent[position] // shards_of).reshape((-1,) + (1,) * (len(extent) - position - 1))

    loudness = one(*cuts[0])
    for cut in cuts[1:]:
        loudness = loudness * one(*cut)
    return loudness


def centred(own_key, shape, deviation, reach, shards=(), kind=jnp.bfloat16):
    drawn = jax.random.normal(own_key, shape, jnp.float32) * deviation
    if len(shards) > 0:
        drawn = level_of(own_key, shape, shards, -0.22, 0.18) * drawn
    return jnp.clip(drawn, min=-reach, max=reach).astype(kind)


def setup_inputs(seed: int = 0) -> dict:
    key_of = jax.random.split(jax.random.key(seed), 16)
    hidden = centred(key_of[0], (SEQS, LEN, D), 1.0, 6.0, ((0, 8), (1, 4)))
    cotangent = centred(key_of[1], (SEQS, LEN, D), 1.0, 6.0, ((0, 8), (1, 4)))
    doc_ids = draw_doc_ids(jax.random.fold_in(key_of[15], 71), 0)
    mixer_in_weight = centred(key_of[3], (D, NIN), D ** -0.5, 0.1875, ((0, 8),))
    mixer_out_weight = centred(key_of[4], (MIXW, D), (MIXW // 8) ** -0.5, 0.375, ((0, 8),))
    feedforward_in_weight = centred(key_of[5], (D, 2 * FF), D ** -0.5, 0.1875, ((0, 8),))
    feedforward_out_weight = centred(key_of[6], (FF, D), FF ** -0.5, 0.125, ((0, 8),))
    gain_in = jnp.clip(1.0 + 0.1 * jax.random.normal(key_of[7], (D,), jnp.float32), 0.5, 1.5).astype(jnp.bfloat16)
    gain_ff = jnp.clip(1.0 + 0.1 * jax.random.normal(key_of[8], (D,), jnp.float32), 0.5, 1.5).astype(jnp.bfloat16)
    gain_mix = jnp.clip(1.0 + 0.1 * jax.random.normal(key_of[9], (MDIM,), jnp.float32), 0.5, 1.5).astype(jnp.bfloat16)
    conv_weight = centred(key_of[10], (CONVC, CONVK), 0.5, 3.0, ((0, 8),))
    conv_bias = jnp.clip(jax.random.uniform(key_of[11], (CONVC,), jnp.float32, -0.5, 0.5) * level_of(key_of[11], (CONVC,), ((0, 8),), -0.4, 0.0), -0.5, 0.5).astype(jnp.bfloat16)
    dt_bias = jnp.clip(jax.random.uniform(key_of[12], (MH,), jnp.float32, -3.0, -1.0), -3.0, -1.0)
    a_log = jnp.clip(jax.random.uniform(key_of[13], (MH,), jnp.float32, -8.0, 1.0), -8.0, 1.0)
    d_skip = jnp.clip(jax.random.uniform(key_of[14], (MH,), jnp.float32, 0.5, 1.5), 0.5, 1.5)
    return {"hidden": hidden, "cotangent": cotangent, "doc_ids": doc_ids, "mixer_in_weight": mixer_in_weight, "mixer_out_weight": mixer_out_weight, "feedforward_in_weight": feedforward_in_weight, "feedforward_out_weight": feedforward_out_weight, "gain_in": gain_in, "gain_ff": gain_ff, "gain_mix": gain_mix, "conv_weight": conv_weight, "conv_bias": conv_bias, "dt_bias": dt_bias, "a_log": a_log, "d_skip": d_skip}


EPS = 1e-05
FULL_PRECISION = lax.Precision.HIGHEST

@jax.custom_vjp
def low(v):
    return lax.optimization_barrier(v.astype(jnp.bfloat16)).astype(jnp.float32)

@jax.custom_vjp
def low_back(v):
    return v

def low_keep(v):
    return (low(v), None)

def low_pass(kept, grad):
    return (grad,)

def back_keep(v):
    return (v, None)

def back_low(kept, grad):
    return (low(grad),)
low.defvjp(low_keep, low_pass)
low_back.defvjp(back_keep, back_low)

def rms_norm(values, gain):
    return values * lax.rsqrt(lax.optimization_barrier(jnp.mean(values * values, -1, keepdims=True)) + EPS) * gain

def rope_tables(positions):
    inverse = 10000.0 ** (-2.0 * jnp.arange(HD // 2, dtype=jnp.float32) / HD)
    angles = positions.astype(jnp.float32)[:, None] * inverse[None, :]
    return (jnp.cos(angles), jnp.sin(angles))

def rotate(values, cos_tab, sin_tab, heads):
    shaped = values.reshape(values.shape[:-1] + (heads, HD))
    first_half = shaped[..., :HD // 2]
    second = shaped[..., HD // 2:]
    cos_b = cos_tab[:, None, :]
    sin_b = sin_tab[:, None, :]
    turned = jnp.concatenate([first_half * cos_b - second * sin_b, second * cos_b + first_half * sin_b], -1)
    return turned.reshape(values.shape)

def conv_apply(extended, weight, bias):
    rows_out = extended.shape[-2] - (CONVK - 1)
    running = bias
    for offset in range(CONVK):
        running = running + weight[:, offset] * extended[..., offset:offset + rows_out, :]
    return running

def mamba_inputs(extended, dt_raw, conv_w, conv_b, dt_bias, a_log):
    activated = jax.nn.silu(conv_apply(extended, conv_w, conv_b))
    x_heads = activated[..., :MDIM].reshape(activated.shape[:-1] + (MH, MP))
    b_in = activated[..., MDIM:MDIM + NSTATE]
    c_out = activated[..., MDIM + NSTATE:]
    dt_val = jax.nn.softplus(dt_raw + dt_bias)
    log_decay = -jnp.exp(a_log) * dt_val
    return (x_heads, b_in, c_out, dt_val, log_decay)

def ssd_stretch(carry_state, pieces):
    x_heads, b_in, c_out, dt_val, log_decay = pieces
    log_cum = jnp.cumsum(log_decay, 0)
    inner_prod = jnp.dot(c_out, b_in.T, precision=FULL_PRECISION)
    log_gaps = log_cum[:, None, :] - log_cum[None, :, :]
    causal = (jnp.arange(STRETCH)[:, None] >= jnp.arange(STRETCH)[None, :])[:, :, None]
    decays = jnp.where(causal, jnp.exp(jnp.where(causal, log_gaps, 0.0)), 0.0)
    mixing = decays * inner_prod[:, :, None] * dt_val[None, :, :]
    local_part = jnp.einsum('tsh,shp->thp', mixing, x_heads, precision=FULL_PRECISION)
    carried = jnp.exp(log_cum)[:, :, None] * jnp.einsum('hpn,tn->thp', carry_state, c_out, precision=FULL_PRECISION)
    weights_s = jnp.exp(log_cum[-1][None, :] - log_cum) * dt_val
    fresh_part = jnp.einsum('shp,sn->hpn', x_heads * weights_s[:, :, None], b_in, precision=FULL_PRECISION)
    new_state = jnp.exp(log_cum[-1])[:, None, None] * carry_state + fresh_part
    return (new_state, local_part + carried)

def ssd_run(x_heads, b_in, c_out, dt_val, log_decay, carry_state):
    blocks = x_heads.shape[0] // STRETCH
    pieces = tuple((member.reshape((blocks, STRETCH) + member.shape[1:]) for member in (x_heads, b_in, c_out, dt_val, log_decay)))
    final_state, outputs = lax.scan(jax.checkpoint(ssd_stretch), carry_state, pieces)
    return (outputs.reshape(x_heads.shape), final_state)

def mamba_tail(y_ssd, x_heads, z_gate, d_skip, gain_mix):
    y_full = y_ssd + d_skip[:, None] * x_heads
    y_flat = y_full.reshape(y_full.shape[:-2] + (MDIM,))
    return rms_norm(y_flat * jax.nn.silu(z_gate), gain_mix)

def attend(queries, keys, values, doc_row):
    length = queries.shape[0]
    q_grp = queries.reshape(length, NHKV, GQ, HD).transpose(1, 2, 0, 3).reshape(NHKV, GQ * length, HD)
    k_grp = keys.reshape(length, NHKV, HD).transpose(1, 0, 2)
    v_grp = values.reshape(length, NHKV, HD).transpose(1, 0, 2)
    scores = low_back(jnp.einsum('hrd,hkd->hrk', q_grp, k_grp, precision=FULL_PRECISION) * (1.0 / math.sqrt(HD)))
    places = jnp.arange(length)
    row_pos = jnp.tile(places, GQ)
    row_doc = jnp.tile(doc_row, GQ)
    allowed = (places[None, :] <= row_pos[:, None]) & (doc_row[None, :] == row_doc[:, None])
    scores = jnp.where(allowed[None], scores, -1e+30)
    highest = lax.optimization_barrier(jnp.max(scores, -1, keepdims=True))
    expo = jnp.exp(scores - highest)
    probs = low(expo / lax.optimization_barrier(jnp.sum(expo, -1, keepdims=True)))
    outputs = jnp.einsum('hrk,hkd->hrd', probs, v_grp, precision=FULL_PRECISION)
    return outputs.reshape(NHKV, GQ, length, HD).transpose(2, 0, 1, 3).reshape(length, ATTW)

def forward(hidden, doc_ids, mixer_in_weight, mixer_out_weight, feedforward_in_weight, feedforward_out_weight, gain_in, gain_ff, gain_mix, conv_weight, conv_bias, dt_bias, a_log, d_skip):
    normalized_input = low(rms_norm(hidden, gain_in))
    projected_rows = low_back(jnp.einsum('ktv,vg->ktg', normalized_input, mixer_in_weight, precision=FULL_PRECISION))
    cos_tab, sin_tab = rope_tables(jnp.arange(LEN))
    queries = low(rotate(projected_rows[..., :ATTW], cos_tab, sin_tab, NHQ))
    keys = low(rotate(projected_rows[..., ATTW:ATTW + KVW], cos_tab, sin_tab, NHKV))
    values = low(projected_rows[..., ATTW + KVW:ATTW + 2 * KVW])
    base = ATTW + 2 * KVW
    z_gate = projected_rows[..., base:base + MDIM]
    conv_in = projected_rows[..., base + MDIM:base + MDIM + CONVC]
    dt_raw = projected_rows[..., base + MDIM + CONVC:]
    attended = lax.map(jax.checkpoint(lambda pieces: attend(pieces[0], pieces[1], pieces[2], pieces[3])), (queries, keys, values, doc_ids))
    extended = jnp.pad(conv_in, ((0, 0), (CONVK - 1, 0), (0, 0)))
    x_heads, b_in, c_out, dt_val, log_decay = mamba_inputs(extended, dt_raw, conv_weight, conv_bias, dt_bias, a_log)
    start_state = jnp.zeros((MH, MP, NSTATE), jnp.float32)
    y_ssd = lax.map(lambda pieces: ssd_run(pieces[0], pieces[1], pieces[2], pieces[3], pieces[4], start_state)[0], (x_heads, b_in, c_out, dt_val, log_decay))
    mamba_out = mamba_tail(y_ssd, x_heads, z_gate, d_skip, gain_mix)
    joined_mixers = low(low_back(jnp.concatenate([attended, mamba_out], -1)))
    middle_hidden = hidden + low_back(jnp.einsum('mue,ek->muk', joined_mixers, mixer_out_weight, precision=FULL_PRECISION))
    normalized_feedforward = low(rms_norm(middle_hidden, gain_ff))
    gate_up_rows = low_back(jnp.einsum('ktv,vg->ktg', normalized_feedforward, feedforward_in_weight, precision=FULL_PRECISION))
    activation_feedforward = low(jax.nn.silu(gate_up_rows[..., :FF]) * gate_up_rows[..., FF:])
    return middle_hidden + low_back(jnp.einsum('mue,ek->muk', activation_feedforward, feedforward_out_weight, precision=FULL_PRECISION))

def reference(hidden, cotangent, doc_ids, mixer_in_weight, mixer_out_weight, feedforward_in_weight, feedforward_out_weight, gain_in, gain_ff, gain_mix, conv_weight, conv_bias, dt_bias, a_log, d_skip):
    params = tuple((param.astype(jnp.float32) for param in (mixer_in_weight, mixer_out_weight, feedforward_in_weight, feedforward_out_weight, gain_in, gain_ff, gain_mix, conv_weight, conv_bias, dt_bias, a_log, d_skip)))
    group = math.gcd(SEQS, max(1, 4096 // LEN))
    groups = SEQS // group

    def one_group(running, pieces):
        hidden_grp, cot_grp, doc_grp = pieces
        out_grp, pull = jax.vjp(lambda hidden_arg, *weights: forward(hidden_arg, doc_grp, *weights), hidden_grp, *params)
        grads = pull(cot_grp)
        running = jax.tree.map(jnp.add, running, tuple(grads[1:]))
        return (running, (out_grp, grads[0]))
    zero_grads = tuple((jnp.zeros_like(param) for param in params))
    totals, (outputs, hidden_grads) = lax.scan(one_group, zero_grads, (hidden.astype(jnp.float32).reshape(groups, group, LEN, D), cotangent.astype(jnp.float32).reshape(groups, group, LEN, D), doc_ids.reshape(groups, group, LEN)))
    return (outputs.reshape(SEQS, LEN, D).astype(jnp.bfloat16), hidden_grads.reshape(SEQS, LEN, D), totals[0], totals[1], totals[2], totals[3], totals[4], totals[5], totals[6], totals[7], totals[8], totals[9], totals[10], totals[11])
```

```python
import functools
import math

import jax
import jax.numpy as jnp
from jax import lax
from jax.experimental import pallas as pl
from jax.experimental.pallas import tpu as pltpu
from jax.sharding import PartitionSpec as P

D = 1024
FF = 2048
NHQ = 8
NHKV = 2
HD = 64
MH = 24
MP = 64
NSTATE = 128
CONVK = 4
GQ = 4
ATTW = 512
KVW = 128
MDIM = 1536
CONVC = 1792
QKV = ATTW + 2 * KVW
NIN = 4120
PAIRS = MH // 2
PW = 2 * MP

EPS = 1e-05
FULL_PRECISION = lax.Precision.HIGHEST
F32 = jnp.float32
BF16 = jnp.bfloat16
VMEM_LIMIT = 48 * 1024 * 1024


def f32(value):
    return value.astype(F32)


def low(value):
    return value.astype(BF16)


def dot_mid(left, right):
    return lax.dot_general(left, right, (((1,), (0,)), ((), ())), preferred_element_type=F32)


def dot_last(left, right):
    return lax.dot_general(left, right, (((1,), (1,)), ((), ())), preferred_element_type=F32)


def dot_first(left, right):
    return lax.dot_general(left, right, (((0,), (0,)), ((), ())), preferred_element_type=F32)


def shifted(value, axis, steps):
    count = lax.axis_size(axis)
    initial, last = (max(0, -steps), min(count, count - steps))
    return lax.ppermute(value, axis, [(source, source + steps) for source in range(initial, last)])


def rope_tables(positions):
    inverse = 10000.0 ** (-2.0 * jnp.arange(HD // 2, dtype=F32) / HD)
    angles = positions.astype(F32)[:, None] * inverse[None, :]
    return (jnp.cos(angles), jnp.sin(angles))


def rotate_heads(shaped, cos_tab, sin_tab):
    first_half = shaped[..., : HD // 2]
    second = shaped[..., HD // 2 :]
    return jnp.concatenate(
        [first_half * cos_tab - second * sin_tab, second * cos_tab + first_half * sin_tab], -1
    )


def heads_first(flat):
    return flat.reshape(flat.shape[0], -1, HD).transpose(1, 0, 2)


def heads_flat(grouped):
    return grouped.transpose(1, 0, 2).reshape(grouped.shape[1], -1)


def att_scores(q_ref, k_ref, keydoc_ref, rowdoc_ref, keypos_ref, rowpos_ref):
    raw = dot_last(q_ref[0], k_ref[0]) * (1.0 / math.sqrt(HD))
    allowed = (keypos_ref[...] <= rowpos_ref[...]) & (keydoc_ref[...] == rowdoc_ref[...])
    return jnp.where(allowed, raw, -1e30)


def att_fwd_kernel(q_ref, k_ref, v_ref, keydoc_ref, rowdoc_ref, keypos_ref, rowpos_ref, o_ref, lse_ref):
    scores = att_scores(q_ref, k_ref, keydoc_ref, rowdoc_ref, keypos_ref, rowpos_ref)
    highest = jnp.max(scores, -1, keepdims=True)
    expo = jnp.exp(scores - highest)
    total = jnp.sum(expo, -1, keepdims=True)
    probs = low(expo * (1.0 / total))
    o_ref[0] = low(dot_mid(probs, v_ref[0]))
    lse_ref[0] = highest + jnp.log(total)


def att_bwd_kernel(
    q_ref, k_ref, v_ref, do_ref, lse_ref, keydoc_ref, rowdoc_ref, keypos_ref, rowpos_ref, *rest
):
    dq_ref, dk_ref, dv_ref = rest[-3:]
    head = pl.program_id(0)
    scores = att_scores(q_ref, k_ref, keydoc_ref, rowdoc_ref, keypos_ref, rowpos_ref)
    probs = jnp.exp(scores - lse_ref[0])
    d_out = do_ref[0]
    d_probs = dot_last(d_out, v_ref[0])
    centre = jnp.sum(probs * d_probs, -1, keepdims=True)
    d_scores = low(probs * (d_probs - centre))
    scale = 1.0 / math.sqrt(HD)
    dq_ref[0] = dot_mid(d_scores, k_ref[0]) * scale
    dk_term = dot_first(d_scores, q_ref[0]) * scale
    dv_term = dot_first(low(probs), d_out)

    @pl.when(head % GQ == 0)
    def _():
        dk_ref[0] = dk_term
        dv_ref[0] = dv_term

    @pl.when(head % GQ != 0)
    def _():
        dk_ref[0] += dk_term
        dv_ref[0] += dv_term


def unread(arrays):
    return [pl.BlockSpec(memory_space=pl.ANY)] * len(arrays)


def att_specs(rows, length):
    whole = lambda shape: pl.BlockSpec(shape, lambda h: (0, 0))
    per_q = pl.BlockSpec((1, rows, HD), lambda h: (h, 0, 0))
    per_kv = pl.BlockSpec((1, length, HD), lambda h: (h // GQ, 0, 0))
    lse = pl.BlockSpec((1, rows, 1), lambda h: (h, 0, 0))
    marks = [whole((1, length)), whole((rows, 1)), whole((1, length)), whole((rows, 1))]
    return per_q, per_kv, lse, marks


def att_cost(rows, length, dots):
    return pl.CostEstimate(
        flops=2 * dots * NHQ * rows * length * HD,
        transcendentals=NHQ * rows * length,
        bytes_accessed=4 * (NHQ * rows + NHKV * length) * HD * 2,
    )


def att_forward(q, k, v, key_doc, row_doc, key_pos, row_pos):
    rows, length = q.shape[1], k.shape[1]
    per_q, per_kv, lse, marks = att_specs(rows, length)
    return pl.pallas_call(
        att_fwd_kernel,
        name="attention_forward",
        grid=(NHQ,),
        in_specs=[per_q, per_kv, per_kv, *marks],
        out_specs=[per_q, lse],
        out_shape=[
            jax.ShapeDtypeStruct((NHQ, rows, HD), BF16),
            jax.ShapeDtypeStruct((NHQ, rows, 1), F32),
        ],
        cost_estimate=att_cost(rows, length, 2),
        compiler_params=pltpu.CompilerParams(vmem_limit_bytes=VMEM_LIMIT),
    )(q, k, v, key_doc, row_doc, key_pos, row_pos)


def att_backward(q, k, v, d_out, log_total, key_doc, row_doc, key_pos, row_pos, earlier):
    rows, length = q.shape[1], k.shape[1]
    per_q, per_kv, lse, marks = att_specs(rows, length)
    return pl.pallas_call(
        att_bwd_kernel,
        name="attention_backward",
        grid=(NHQ,),
        in_specs=[per_q, per_kv, per_kv, per_q, lse, *marks, *unread(earlier)],
        out_specs=[per_q, per_kv, per_kv],
        out_shape=[
            jax.ShapeDtypeStruct((NHQ, rows, HD), F32),
            jax.ShapeDtypeStruct((NHKV, length, HD), F32),
            jax.ShapeDtypeStruct((NHKV, length, HD), F32),
        ],
        cost_estimate=att_cost(rows, length, 5),
        compiler_params=pltpu.CompilerParams(vmem_limit_bytes=VMEM_LIMIT),
    )(q, k, v, d_out, log_total, key_doc, row_doc, key_pos, row_pos, *earlier)


def column_of(table, head):
    lanes = lax.broadcasted_iota(jnp.int32, table.shape, 1)
    return jnp.sum(jnp.where(lanes == head, table, 0.0), 1, keepdims=True)


def decay_matrix(cum_ref, cumt_ref, head):
    column = column_of(cum_ref[...], head)
    row = cumt_ref[pl.ds(head, 1), :]
    rows = column.shape[0]
    at = lax.broadcasted_iota(jnp.int32, (rows, rows), 0)
    source = lax.broadcasted_iota(jnp.int32, (rows, rows), 1)
    return column, row, jnp.exp(jnp.where(at >= source, column - row, -1e30))


def first_half_lanes(shape):
    return lax.broadcasted_iota(jnp.int32, shape, 1) < MP


def ssd_fwd_kernel(
    x_ref, b_ref, c_ref, dt_ref, cum_ref, dtt_ref, cumt_ref, y_ref, state_ref, inner
):
    pair = pl.program_id(0)
    b_in = low(b_ref[...])

    @pl.when(pair == 0)
    def _():
        inner[...] = dot_last(low(c_ref[...]), b_in)

    x_pair = x_ref[...]
    x_low = low(x_pair)
    parts, weights = [], []
    for i in range(2):
        head = 2 * pair + i
        column, row, decays = decay_matrix(cum_ref, cumt_ref, head)
        mixing = low(decays * inner[...] * dtt_ref[pl.ds(head, 1), :])
        parts.append(dot_mid(mixing, x_low))
        rows = column.shape[0]
        weights.append(jnp.exp(row[:, rows - 1 :] - column) * column_of(dt_ref[...], head))
    left = first_half_lanes(x_pair.shape)
    y_ref[...] = jnp.where(left, parts[0], parts[1])
    weighted = low(x_pair * jnp.where(left, weights[0], weights[1]))
    state_ref[...] = low(dot_first(weighted, b_in))


def ssd_bwd_kernel(
    x_ref, b_ref, c_ref, dy_ref, cum_ref, dtt_ref, cumt_ref, *rest
):
    dx_ref, db_ref, dc_ref, inner, d_inner = rest[-5:]
    pair = pl.program_id(0)
    b_in = low(b_ref[...])
    c_out = low(c_ref[...])

    @pl.when(pair == 0)
    def _():
        inner[...] = dot_last(c_out, b_in)
        d_inner[...] = jnp.zeros_like(d_inner)

    x_low = low(x_ref[...])
    dy_low = low(dy_ref[...])
    left = first_half_lanes(x_low.shape)
    parts = []
    for i in range(2):
        head = 2 * pair + i
        _, _, decays = decay_matrix(cum_ref, cumt_ref, head)
        scaled = decays * dtt_ref[pl.ds(head, 1), :]
        mixing = low(scaled * inner[...])
        parts.append(dot_first(mixing, dy_low))
        mine = left if i == 0 else jnp.logical_not(left)
        d_mixing = dot_last(jnp.where(mine, dy_low, jnp.zeros_like(dy_low)), x_low)
        d_inner[...] += d_mixing * scaled
    dx_ref[...] = jnp.where(left, parts[0], parts[1])

    @pl.when(pair == PAIRS - 1)
    def _():
        d_low = low(d_inner[...])
        dc_ref[...] = dot_mid(d_low, b_in)
        db_ref[...] = dot_first(d_low, c_out)


def ssd_join_kernel(
    x_ref, b_ref, dxl_ref, dy_ref, y_ref, state_ref, dstate_ref, dt_ref, cum_ref, cumt_ref,
    dbl_ref, dcl_ref, *rest,
):
    dx_ref, db_ref, dc_ref, row_ref, coll_ref, cols_ref, edge_ref = rest[-7:]
    pair = pl.program_id(0)
    x_pair = x_ref[...]
    left = first_half_lanes(x_pair.shape)
    rows = x_pair.shape[0]

    @pl.when(pair == 0)
    def _():
        db_ref[...] = dbl_ref[...]
        dc_ref[...] = dcl_ref[...]
        row_ref[...] = jnp.zeros_like(row_ref)
        coll_ref[...] = jnp.zeros_like(coll_ref)
        cols_ref[...] = jnp.zeros_like(cols_ref)
        edge_ref[...] = jnp.zeros_like(edge_ref)

    weights, growth, ends = [], [], []
    for i in range(2):
        head = 2 * pair + i
        column = column_of(cum_ref[...], head)
        end = cumt_ref[pl.ds(head, 1), :][:, rows - 1 :]
        weights.append(jnp.exp(end - column) * column_of(dt_ref[...], head))
        growth.append(jnp.exp(column))
        ends.append(jnp.exp(end))
    weight = jnp.where(left, weights[0], weights[1])
    grown = jnp.where(left, growth[0], growth[1])
    state = state_ref[...]
    d_state = dstate_ref[...]
    d_y = dy_ref[...]
    x_low = low(x_pair)
    weighted = low(x_pair * weight)
    through = dot_last(low(b_ref[...]), d_state)
    dx_ref[...] = dxl_ref[...] + weight * through
    db_ref[...] += dot_mid(weighted, d_state)
    dc_ref[...] += dot_mid(low(d_y * grown), state)
    row_term = f32(low(d_y)) * y_ref[...]
    local_term = f32(x_low) * dxl_ref[...]
    state_term = f32(weighted) * through
    met = f32(state) * f32(d_state)
    lanes = lax.broadcasted_iota(jnp.int32, row_ref.shape, 1)
    edge_lanes = lax.broadcasted_iota(jnp.int32, edge_ref.shape, 1)
    for i in range(2):
        mine = left if i == 0 else jnp.logical_not(left)
        here = lanes == 2 * pair + i
        for ref, term in ((row_ref, row_term), (coll_ref, local_term), (cols_ref, state_term)):
            total = jnp.sum(jnp.where(mine, term, 0.0), 1, keepdims=True)
            ref[...] = jnp.where(here, total, ref[...])
        half = met[i * MP : (i + 1) * MP]
        across = jnp.sum(jnp.sum(half, 1, keepdims=True), 0, keepdims=True) * ends[i]
        edge_ref[...] = jnp.where(edge_lanes == 2 * pair + i, across, edge_ref[...])


def ssd_cost(rows, dots, width):
    return pl.CostEstimate(
        flops=2 * dots * MH * rows * rows * PW,
        transcendentals=MH * rows * rows,
        bytes_accessed=4 * rows * MDIM * width,
    )


def ssd_specs(rows):
    pair_of = pl.BlockSpec((rows, PW), lambda p: (0, p))
    b_of = pl.BlockSpec((rows, NSTATE), lambda p: (0, PAIRS))
    c_of = pl.BlockSpec((rows, NSTATE), lambda p: (0, PAIRS + 1))
    once = pl.BlockSpec((rows, NSTATE), lambda p: (0, 0))
    tall = pl.BlockSpec((rows, MH), lambda p: (0, 0))
    wide = pl.BlockSpec((MH, rows), lambda p: (0, 0))
    state = pl.BlockSpec((PW, NSTATE), lambda p: (p, 0))
    return pair_of, b_of, c_of, once, tall, wide, state


def ssd_forward(act, dt_val, cum, dt_turned, cum_turned):
    rows = act.shape[0]
    pair_of, b_of, c_of, _, tall, wide, state = ssd_specs(rows)
    return pl.pallas_call(
        ssd_fwd_kernel,
        name="ssd_forward",
        grid=(PAIRS,),
        in_specs=[pair_of, b_of, c_of, tall, tall, wide, wide],
        out_specs=[pair_of, state],
        out_shape=[
            jax.ShapeDtypeStruct((rows, MDIM), F32),
            jax.ShapeDtypeStruct((MDIM, NSTATE), BF16),
        ],
        scratch_shapes=[pltpu.VMEM((rows, rows), F32)],
        cost_estimate=ssd_cost(rows, 1, 2),
        compiler_params=pltpu.CompilerParams(vmem_limit_bytes=VMEM_LIMIT),
    )(act, act, act, dt_val, cum, dt_turned, cum_turned)


def ssd_backward(act, d_y, cum, dt_turned, cum_turned, earlier):
    rows = act.shape[0]
    pair_of, b_of, c_of, once, tall, wide, _ = ssd_specs(rows)
    return pl.pallas_call(
        ssd_bwd_kernel,
        name="ssd_backward",
        grid=(PAIRS,),
        in_specs=[pair_of, b_of, c_of, pair_of, tall, wide, wide, *unread(earlier)],
        out_specs=[pair_of, once, once],
        out_shape=[
            jax.ShapeDtypeStruct((rows, MDIM), F32),
            jax.ShapeDtypeStruct((rows, NSTATE), F32),
            jax.ShapeDtypeStruct((rows, NSTATE), F32),
        ],
        scratch_shapes=[pltpu.VMEM((rows, rows), F32), pltpu.VMEM((rows, rows), F32)],
        cost_estimate=ssd_cost(rows, 2, 3),
        compiler_params=pltpu.CompilerParams(vmem_limit_bytes=VMEM_LIMIT),
    )(act, act, act, d_y, cum, dt_turned, cum_turned, *earlier)


def ssd_join(
    act, dx_local, d_y, y_ssd, state, d_state, dt_val, cum, cum_turned, db_local, dc_local, earlier
):
    rows = act.shape[0]
    pair_of, b_of, _, once, tall, wide, state_of = ssd_specs(rows)
    edge = pl.BlockSpec((1, MH), lambda p: (0, 0))
    return pl.pallas_call(
        ssd_join_kernel,
        name="ssd_join",
        grid=(PAIRS,),
        in_specs=[
            pair_of, b_of, pair_of, pair_of, pair_of, state_of, state_of, tall, tall, wide,
            once, once, *unread(earlier),
        ],
        out_specs=[pair_of, once, once, tall, tall, tall, edge],
        out_shape=[
            jax.ShapeDtypeStruct((rows, MDIM), F32),
            jax.ShapeDtypeStruct((rows, NSTATE), F32),
            jax.ShapeDtypeStruct((rows, NSTATE), F32),
            jax.ShapeDtypeStruct((rows, MH), F32),
            jax.ShapeDtypeStruct((rows, MH), F32),
            jax.ShapeDtypeStruct((rows, MH), F32),
            jax.ShapeDtypeStruct((1, MH), F32),
        ],
        cost_estimate=pl.CostEstimate(
            flops=6 * rows * MDIM * NSTATE,
            transcendentals=3 * rows * MH,
            bytes_accessed=4 * rows * MDIM * 5,
        ),
        compiler_params=pltpu.CompilerParams(vmem_limit_bytes=VMEM_LIMIT),
    )(
        act, act, dx_local, d_y, y_ssd, state, d_state, dt_val, cum, cum_turned, db_local, dc_local,
        *earlier,
    )


STEPS = 4


def square_of(ref):
    block = ref[...]
    return block.reshape(block.shape[0] * block.shape[1], block.shape[2])


def call_ffn(kernel, name, in_specs, out_specs, out_shape, flops, operands, scratch=()):
    return pl.pallas_call(
        kernel,
        name=name,
        grid=(STEPS,),
        in_specs=in_specs,
        out_specs=out_specs,
        out_shape=out_shape,
        scratch_shapes=list(scratch),
        cost_estimate=pl.CostEstimate(flops=flops, transcendentals=0, bytes_accessed=flops // 256),
        compiler_params=pltpu.CompilerParams(vmem_limit_bytes=VMEM_LIMIT),
    )(*operands)


def whole_of(shape):
    return pl.BlockSpec(shape, lambda k: (0,) * len(shape))


def column_block(rows, width):
    return pl.BlockSpec((rows, width), lambda k: (0, k))


def devices_block(stack, part):
    count, tall, _ = stack.shape
    return pl.BlockSpec((count // STEPS, tall // 4, D), lambda k: (k, part, 0))


def middle_kernel(hidden_ref, joined_ref, w_ref, gain_ref, middle_ref, ff_ref, scale_ref):
    step = pl.program_id(0)
    term = dot_mid(joined_ref[...], square_of(w_ref))

    @pl.when(step == 0)
    def _():
        middle_ref[...] = f32(hidden_ref[...]) + term

    @pl.when(step != 0)
    def _():
        middle_ref[...] += term

    @pl.when(step == STEPS - 1)
    def _():
        middle = middle_ref[...]
        scale = lax.rsqrt(jnp.mean(middle * middle, -1, keepdims=True) + EPS)
        scale_ref[...] = scale
        ff_ref[...] = low(middle * scale * gain_ref[...])


def ffn_middle(hidden, joined, stack, gain):
    rows, width = joined.shape
    return call_ffn(
        middle_kernel,
        "middle",
        [
            whole_of((rows, D)),
            column_block(rows, width // STEPS),
            devices_block(stack, 2),
            whole_of((1, D)),
        ],
        [whole_of((rows, D)), whole_of((rows, D)), whole_of((rows, 1))],
        [
            jax.ShapeDtypeStruct((rows, D), F32),
            jax.ShapeDtypeStruct((rows, D), BF16),
            jax.ShapeDtypeStruct((rows, 1), F32),
        ],
        2 * rows * width * D,
        (hidden, joined, stack, gain),
    )


def gate_kernel(ff_ref, gate_w_ref, up_w_ref, gate_ref, up_ref, act_ref):
    ff = ff_ref[...]
    gate = dot_mid(ff, square_of(gate_w_ref))
    up = dot_mid(ff, square_of(up_w_ref))
    gate_ref[...] = gate
    up_ref[...] = up
    act_ref[...] = low(gate * jax.nn.sigmoid(gate) * up)


def ffn_gate(ff, stack):
    rows = ff.shape[0]
    count, tall, _ = stack.shape
    quarter = lambda first: pl.BlockSpec(
        (count, tall // 8, D // 2), lambda k: (0, first + k // 2, k % 2)
    )
    out = column_block(rows, FF // STEPS)
    return call_ffn(
        gate_kernel,
        "gate_up",
        [whole_of((rows, D)), quarter(0), quarter(2)],
        [out, out, out],
        [
            jax.ShapeDtypeStruct((rows, FF), F32),
            jax.ShapeDtypeStruct((rows, FF), F32),
            jax.ShapeDtypeStruct((rows, FF), BF16),
        ],
        4 * rows * FF * D,
        (ff, stack, stack),
    )


def output_kernel(middle_ref, act_ref, w_ref, *rest):
    out_ref, total = rest[-2:]
    step = pl.program_id(0)
    term = dot_mid(act_ref[...], square_of(w_ref))

    @pl.when(step == 0)
    def _():
        total[...] = middle_ref[...] + term

    @pl.when(step != 0)
    def _():
        total[...] += term

    @pl.when(step == STEPS - 1)
    def _():
        out_ref[...] = low(total[...])


def ffn_output(middle, act, stack, earlier):
    rows, width = act.shape
    return call_ffn(
        output_kernel,
        "layer_output",
        [
            whole_of((rows, D)),
            column_block(rows, width // STEPS),
            devices_block(stack, 3),
            *unread(earlier),
        ],
        whole_of((rows, D)),
        jax.ShapeDtypeStruct((rows, D), BF16),
        2 * rows * width * D,
        (middle, act, stack, *earlier),
        [pltpu.VMEM((rows, D), F32)],
    )


def d_gate_kernel(cot_ref, w_ref, gate_ref, up_ref, *rest):
    d_ref = rest[-1]
    step = pl.program_id(0)
    width = gate_ref.shape[1]
    d_act = dot_last(cot_ref[...], square_of(w_ref))
    gate = gate_ref[...]
    sigma = jax.nn.sigmoid(gate)
    start = pl.multiple_of(step * width, 128)
    d_ref[:, pl.ds(start, width)] = low(d_act * up_ref[...] * silu_slope(gate, sigma))
    d_ref[:, pl.ds(start + FF, width)] = low(d_act * (gate * sigma))


def ffn_d_gate(cot, stack, gate, up, earlier):
    rows = cot.shape[0]
    block = column_block(rows, FF // STEPS)
    return call_ffn(
        d_gate_kernel,
        "d_gate_up",
        [whole_of((rows, D)), devices_block(stack, 3), block, block, *unread(earlier)],
        whole_of((rows, 2 * FF)),
        jax.ShapeDtypeStruct((rows, 2 * FF), BF16),
        2 * rows * FF * D,
        (cot, stack, gate, up, *earlier),
    )


def d_middle_kernel(d_gu_ref, w_ref, middle_ref, scale_ref, gain_ref, cot_ref, *rest):
    d_ref, low_ref, gain_grad_ref = rest[-3:]
    step = pl.program_id(0)
    term = dot_last(d_gu_ref[...], square_of(w_ref))

    @pl.when(step == 0)
    def _():
        d_ref[...] = term

    @pl.when(step != 0)
    def _():
        d_ref[...] += term

    @pl.when(step == STEPS - 1)
    def _():
        d_normed = d_ref[...]
        scale = scale_ref[...]
        unit = middle_ref[...] * scale
        gain_grad_ref[...] = jnp.sum(d_normed * unit, 0, keepdims=True)
        d_unit = d_normed * gain_ref[...]
        inner = jnp.mean(d_unit * unit, -1, keepdims=True)
        d_middle = f32(cot_ref[...]) + scale * (d_unit - unit * inner)
        d_ref[...] = d_middle
        low_ref[...] = low(d_middle)


def ffn_d_middle(d_gu, stack, middle, scale, gain, cot, earlier):
    rows = d_gu.shape[0]
    count, tall, _ = stack.shape
    whole = whole_of((rows, D))
    return call_ffn(
        d_middle_kernel,
        "d_middle",
        [
            column_block(rows, D),
            pl.BlockSpec((count, tall // 8, D), lambda k: (0, k, 0)),
            whole,
            whole_of((rows, 1)),
            whole_of((1, D)),
            whole,
            *unread(earlier),
        ],
        [whole, whole, whole_of((1, D))],
        [
            jax.ShapeDtypeStruct((rows, D), F32),
            jax.ShapeDtypeStruct((rows, D), BF16),
            jax.ShapeDtypeStruct((1, D), F32),
        ],
        4 * rows * FF * D,
        (d_gu, stack, middle, scale, gain, cot, *earlier),
    )


def d_joined_kernel(d_ref, w_ref, out_ref):
    out_ref[...] = low(dot_last(d_ref[...], square_of(w_ref)))


def mixer_d_joined(d_middle, stack):
    rows = d_middle.shape[0]
    width = 2 * D
    return call_ffn(
        d_joined_kernel,
        "d_joined",
        [whole_of((rows, D)), devices_block(stack, 2)],
        column_block(rows, width // STEPS),
        jax.ShapeDtypeStruct((rows, width), BF16),
        2 * rows * width * D,
        (d_middle, stack),
    )


def flipped(value, bit):
    count = lax.axis_size("fsdp")
    return lax.ppermute(value, "fsdp", [(i, i ^ bit) for i in range(count)])


def squares():
    return lax.axis_size("fsdp") == 8


def gather_rows(shard):
    return lax.all_gather(shard, "fsdp", axis=0, tiled=True)


def device_columns(left, flips, depth, offset):
    count = lax.axis_size("fsdp")
    stride = left.shape[1] // count
    me = lax.axis_index("fsdp")
    return jnp.concatenate(
        [
            lax.dynamic_slice_in_dim(left, (me ^ flip) * stride + offset, depth, 1)
            for flip in flips
        ],
        1,
    )


def scatter_products(products, depth, flips):
    return jnp.concatenate(
        [dot_first(device_columns(left, flips, depth, at), right) for left, at, right in products],
        1,
    )


def scatter_open(products, depth):
    if squares():
        return low(scatter_products(products, depth, (1, 3, 5, 7)))
    count = lax.axis_size("fsdp")
    whole = []
    for left, at, right in products:
        rows = left.reshape(left.shape[0], count, -1)[:, :, at : at + depth]
        whole.append(low(dot_first(rows.reshape(left.shape[0], -1), right)))
    return lax.psum_scatter(
        jnp.concatenate(whole, 1), "fsdp", scatter_dimension=0, tiled=True
    )


def scatter_swap(products, depth, theirs):
    if not squares():
        return theirs
    ours = scatter_products(products, depth, (0, 2, 4, 6))
    return low(ours + f32(flipped(theirs, 1))).reshape(4, depth, -1)


def scatter_first(ours):
    if not squares():
        return ours, ours
    half = ours.shape[1] // 2
    for_y = flipped(ours[3, :half], 2)
    for_x = flipped(ours[3, half:], 4)
    to_x = jnp.concatenate([ours[1, :half], low(f32(ours[1, half:]) + f32(for_x))], 0)
    to_y = jnp.concatenate([low(f32(ours[2, :half]) + f32(for_y)), ours[2, half:]], 0)
    return to_x, to_y


def scatter_last(ours, to_x, to_y):
    if not squares():
        return ours
    return low(f32(ours[0]) + f32(flipped(to_x, 2)) + f32(flipped(to_y, 4)))


def grid_total(value):
    if not squares() or lax.axis_size("ctx") != 4:
        return lax.psum(value, ("ctx", "fsdp"))
    for bit in (1, 2, 4):
        value = value + flipped(value, bit)
    for bit in (1, 2):
        value = value + ctx_flipped(value, bit)
    return value


def ctx_flipped(value, bit):
    return lax.ppermute(value, "ctx", [(i, i ^ bit) for i in range(lax.axis_size("ctx"))])


def ctx_total(part):
    if lax.axis_size("ctx") != 4:
        return f32(lax.psum(part, "ctx"))
    me = lax.axis_index("ctx")
    value = part
    for bit in (1, 2):
        size = value.shape[0] // 2
        upper = (me // bit) % 2
        mine = lax.dynamic_slice_in_dim(value, upper * size, size, 0)
        theirs = lax.dynamic_slice_in_dim(value, (1 - upper) * size, size, 0)
        value = low(f32(mine) + f32(ctx_flipped(theirs, bit)))
    for bit in (2, 1):
        upper = (me // bit) % 2
        other = ctx_flipped(value, bit)
        value = jnp.concatenate(
            [jnp.where(upper == 0, value, other), jnp.where(upper == 0, other, value)], 0
        )
    return f32(value)


def entering(own, decay, direction):
    count = lax.axis_size("ctx")
    coarse = low(decay)
    fine = low(decay - f32(coarse))
    line = jnp.concatenate([coarse, fine, jnp.zeros((NSTATE - 2 * MH,), BF16)])
    packed = jnp.concatenate([own, jnp.broadcast_to(line[None], (16, NSTATE))], 0)
    total = jnp.zeros(own.shape, F32)
    carried = jnp.ones(decay.shape, F32)
    for distance in range(1, count):
        came = shifted(packed, "ctx", direction * distance)
        total = total + f32(came[:MDIM]) * jnp.repeat(carried, MP)[:, None]
        line = f32(came[MDIM])
        carried = carried * (line[:MH] + line[MH : 2 * MH])
    return total


def after(value, earlier):
    return lax.optimization_barrier((value, earlier))[0]


def silu_slope(value, sigma):
    return sigma * (1.0 + value * (1.0 - sigma))


def body(
    hidden,
    cotangent,
    doc_ids,
    mixer_in_weight,
    mixer_out_weight,
    feedforward_in_weight,
    feedforward_out_weight,
    gain_in,
    gain_ff,
    gain_mix,
    conv_weight,
    conv_bias,
    dt_bias,
    a_log,
    d_skip,
):
    rows = hidden.shape[1]
    shards = lax.axis_size("fsdp")

    small = [gain_in, gain_ff, gain_mix, conv_weight.T.reshape(-1), conv_bias]
    sizes = [piece.shape[0] for piece in small]
    depth = mixer_in_weight.shape[0]
    lines = -(-sum(sizes) // depth)
    line = jnp.concatenate(small + [jnp.zeros((lines * depth - sum(sizes),), BF16)])
    full_in = gather_rows(
        jnp.concatenate([mixer_in_weight, line.reshape(lines, depth).T], 1)
    )
    full_qkv = full_in[:, :QKV]
    full_z = full_in[:, QKV : QKV + MDIM]
    full_cd = full_in[:, QKV + MDIM : NIN]

    small_all = f32(full_in[:, NIN:]).T.reshape(lines, shards, depth)
    small_all = small_all.transpose(1, 0, 2).reshape(shards, lines * depth)
    cuts = [sum(sizes[:i]) for i in range(len(sizes) + 1)]
    gin, gff, gmix, convw, convb = [
        small_all[:, cuts[i] : cuts[i + 1]] for i in range(len(sizes))
    ]
    gin, gff, gmix, convb = [piece.reshape(-1) for piece in (gin, gff, gmix, convb)]
    convw = convw.reshape(shards, CONVK, -1).transpose(1, 0, 2).reshape(CONVK, CONVC)

    quarters = [feedforward_in_weight[:, i * D : (i + 1) * D] for i in range(4)]
    stack = lax.all_gather(
        jnp.concatenate([*quarters, mixer_out_weight, feedforward_out_weight], 0), "fsdp", axis=0
    )

    hidden32 = f32(hidden[0])
    scale_in = lax.rsqrt(jnp.mean(hidden32 * hidden32, -1, keepdims=True) + EPS)
    normed_b = low(hidden32 * scale_in * gin)

    proj_cd = dot_mid(normed_b, full_cd)
    conv_in = proj_cd[:, :CONVC]
    dt_raw = proj_cd[:, CONVC:]
    rim = shifted(conv_in[rows - (CONVK - 1) :], "ctx", 1)
    extended = jnp.concatenate([rim, conv_in], 0)
    u = convb
    for tap in range(CONVK):
        u = u + convw[tap] * extended[tap : tap + rows]
    u_sigma = jax.nn.sigmoid(u)
    act = u * u_sigma
    dt_arg = dt_raw + dt_bias
    dt_val = jax.nn.softplus(dt_arg)
    rate = -jnp.exp(a_log)
    log_decay = rate * dt_val
    ones = (jnp.arange(rows)[:, None] >= jnp.arange(rows)[None, :]).astype(F32)
    cum = lax.dot_general(ones, log_decay, (((1,), (0,)), ((), ())), precision=FULL_PRECISION)
    cum_turned = cum.T
    dt_turned = dt_val.T
    y_local, own_state = ssd_forward(act, dt_val, cum, dt_turned, cum_turned)
    own_decay = jnp.exp(cum[-1])

    proj_qkv = dot_mid(normed_b, full_qkv)
    positions = lax.axis_index("ctx") * rows + jnp.arange(rows)
    cos_tab, sin_tab = rope_tables(positions)
    q_heads = low(rotate_heads(heads_first(proj_qkv[:, :ATTW]), cos_tab, sin_tab))
    k_heads = low(rotate_heads(heads_first(proj_qkv[:, ATTW : ATTW + KVW]), cos_tab, sin_tab))
    v_heads = low(heads_first(proj_qkv[:, ATTW + KVW :]))
    doc_here = low(doc_ids[0])
    doc_line = jnp.concatenate([doc_here, jnp.zeros((2 * KVW - rows,), BF16)])
    own_kv = jnp.concatenate(
        [
            jnp.concatenate([heads_flat(k_heads), heads_flat(v_heads)], 1),
            jnp.broadcast_to(doc_line[None], (16, 2 * KVW)),
        ],
        0,
    )
    blocks = lax.axis_size("ctx")
    me = lax.axis_index("ctx")
    came = [own_kv] + [shifted(own_kv, "ctx", distance) for distance in range(1, blocks)]
    kv_all = jnp.concatenate([block[:rows] for block in came], 0)
    k_all = heads_first(kv_all[:, :KVW])
    v_all = heads_first(kv_all[:, KVW:])
    key_doc = jnp.concatenate([block[rows, :rows] for block in came])[None, :].astype(jnp.int32)
    row_doc = doc_ids[0][:, None]
    row_pos = positions.astype(jnp.int32)[:, None]
    key_pos = jnp.concatenate(
        [
            jnp.where(me >= distance, positions - distance * rows, blocks * rows)
            for distance in range(blocks)
        ]
    )[None, :]
    attended, log_total = att_forward(q_heads, k_all, v_all, key_doc, row_doc, key_pos, row_pos)

    state_in = low(entering(own_state, own_decay, 1))
    spread = (jnp.arange(MH)[:, None] == (jnp.arange(MDIM) // MP)[None, :]).astype(F32)
    grown = lax.dot_general(
        jnp.exp(cum), spread, (((1,), (0,)), ((), ())), precision=FULL_PRECISION
    )
    x_flat = act[:, :MDIM]
    c_low = low(act[:, MDIM + NSTATE :])
    y_ssd = y_local + grown * dot_last(c_low, state_in)
    z_gate = dot_mid(normed_b, full_z)
    skip = jnp.repeat(d_skip, MP)
    y_full = y_ssd + skip * x_flat
    z_sigma = jax.nn.sigmoid(z_gate)
    z_act = z_gate * z_sigma
    gated = y_full * z_act
    scale_mix = lax.rsqrt(jnp.mean(gated * gated, -1, keepdims=True) + EPS)
    joined_b = jnp.concatenate(
        [heads_flat(attended), low(gated * scale_mix * gmix)], 1
    )

    cot_b = cotangent[0]
    middle, ff_b, scale_ff = ffn_middle(hidden[0], joined_b, stack, gff[None])
    gate_val, up_val, act_b = ffn_gate(ff_b, stack)

    grad_fo = low(dot_first(act_b, cot_b))
    part_fo = lax.psum_scatter(grad_fo, "fsdp", scatter_dimension=0, tiled=True)
    d_gu = ffn_d_gate(cot_b, stack, gate_val, up_val, [grad_fo])
    grad_fi = low(dot_first(ff_b, d_gu))
    part_fi = lax.psum_scatter(grad_fi, "fsdp", scatter_dimension=0, tiled=True)
    d_middle, d_middle_b, dg_ff = ffn_d_middle(
        d_gu, stack, middle, scale_ff, gff[None], cot_b, [grad_fi]
    )
    dg_ff = dg_ff[0]
    d_joined = mixer_d_joined(d_middle_b, stack)
    d_mamba = f32(d_joined[:, ATTW:])
    unit_mix = gated * scale_mix
    dg_mix = jnp.sum(d_mamba * unit_mix, 0)
    d_unit_mix = d_mamba * gmix
    d_gated = scale_mix * (
        d_unit_mix - unit_mix * jnp.mean(d_unit_mix * unit_mix, -1, keepdims=True)
    )
    d_y = d_gated * z_act
    d_z = low(d_gated * y_full * silu_slope(z_gate, z_sigma))
    dd_skip = jnp.sum(jnp.sum(d_y * x_flat, 0).reshape(MH, MP), 1)
    local_grad = low(dot_first(low(d_y * grown), c_low))

    group_m = [(joined_b, 0, d_middle_b), (joined_b, depth, d_middle_b), (normed_b, 0, d_z)]
    theirs_m = scatter_open(group_m, depth)

    dx_local, db_local, dc_local = ssd_backward(
        act, d_y, cum, dt_turned, cum_turned, [theirs_m, local_grad]
    )
    d_state = low(entering(local_grad, own_decay, -1))
    ours_m = scatter_swap(group_m, depth, theirs_m)
    do_heads = heads_first(d_joined[:, :ATTW])
    d_q, d_k, d_v = att_backward(
        q_heads, k_all, v_all, do_heads, log_total, key_doc, row_doc, key_pos, row_pos,
        [ours_m, dx_local],
    )
    to_x_m, to_y_m = scatter_first(ours_m)
    result = ffn_output(middle, act_b, stack, [d_q])
    d_kv = jnp.concatenate([heads_flat(d_k), heads_flat(d_v)], 1)
    terms = low(d_kv[rows:])
    terms = after(terms, (d_state, result))
    dx_ssd, d_b, d_c, row_term, col_local, col_state, edge = ssd_join(
        act, dx_local, d_y, y_ssd, state_in, d_state, dt_val, cum, cum_turned, db_local, dc_local,
        [to_x_m, to_y_m, part_fo, terms],
    )
    received = [
        shifted(terms[(distance - 1) * rows : distance * rows], "ctx", -distance)
        for distance in range(1, blocks)
    ]
    received, dx_ssd = lax.optimization_barrier((received, dx_ssd))
    dkv = d_kv[:rows] + sum(f32(term) for term in received)
    d_q = rotate_heads(d_q, cos_tab, -sin_tab)
    d_k = rotate_heads(heads_first(dkv[:, :KVW]), cos_tab, -sin_tab)
    d_qkv = jnp.concatenate([low(heads_flat(d_q)), low(heads_flat(d_k)), low(dkv[:, KVW:])], 1)
    part_m = scatter_last(ours_m, to_x_m, to_y_m)

    col_term = col_local + col_state
    d_cum = row_term - col_term
    d_end = jnp.sum(col_state, 0) + edge[0]
    d_decay = (
        lax.dot_general(ones, d_cum, (((0,), (0,)), ((), ())), precision=FULL_PRECISION) + d_end
    )
    d_alog = jnp.sum(d_decay * log_decay, 0)
    dt_sigma = jax.nn.sigmoid(dt_arg)
    ratio = jnp.where(dt_arg < -30.0, 1.0, dt_sigma / jnp.where(dt_arg < -30.0, 1.0, dt_val))
    d_dtraw = col_term * ratio + d_decay * rate * dt_sigma
    d_dtbias = jnp.sum(d_dtraw, 0)

    d_act_conv = jnp.concatenate([dx_ssd + skip * d_y, d_b, d_c], 1)
    d_u = d_act_conv * silu_slope(u, u_sigma)
    d_convb = jnp.sum(d_u, 0)
    d_convw = jnp.stack(
        [jnp.sum(d_u * extended[tap : tap + rows], 0) for tap in range(CONVK)]
    )
    d_u_ext = jnp.concatenate([d_u, shifted(d_u[: CONVK - 1], "ctx", -1)], 0)
    d_conv_in = sum(
        convw[tap] * d_u_ext[CONVK - 1 - tap : CONVK - 1 - tap + rows] for tap in range(CONVK)
    )
    d_cd = jnp.concatenate([low(d_conv_in), low(d_dtraw)], 1)
    group_c = [(normed_b, 0, d_qkv), (normed_b, 0, d_cd)]
    theirs_c = scatter_open(group_c, depth)
    ours_c = scatter_swap(group_c, depth, theirs_c)
    ours_c = after(ours_c, part_m)
    to_x_c, to_y_c = scatter_first(ours_c)
    to_x_c = after(to_x_c, part_fi)
    part_c = scatter_last(ours_c, to_x_c, to_y_c)

    d_normed = dot_last(d_cd, full_cd) + dot_last(d_qkv, full_qkv) + dot_last(d_z, full_z)
    unit_in = hidden32 * scale_in
    dg_in = jnp.sum(d_normed * unit_in, 0)
    d_unit_in = d_normed * gin
    d_hidden = d_middle + scale_in * (
        d_unit_in - unit_in * jnp.mean(d_unit_in * unit_in, -1, keepdims=True)
    )

    tot_fo = f32(lax.psum(part_fo, "ctx"))
    tot_fi = f32(lax.psum(part_fi, "ctx"))
    tot_m = ctx_total(part_m)
    tot_c = ctx_total(part_c)
    tot_mo = jnp.concatenate([tot_m[:, :D], tot_m[:, D : 2 * D]], 0)
    small_grads = jnp.concatenate(
        [dg_in, dg_ff, dg_mix, d_convw.reshape(-1), d_convb, d_dtbias, d_alog, dd_skip]
    )
    small_total = grid_total(small_grads)
    mine = lax.axis_index("fsdp")
    place = 0

    def own_part(width, count=1):
        nonlocal place
        block = small_total[place : place + width * count].reshape(count, width)
        place += width * count
        return lax.dynamic_slice_in_dim(block, mine * (width // shards), width // shards, 1)

    tg_in = own_part(D)[0]
    tg_ff = own_part(D)[0]
    tg_mix = own_part(MDIM)[0]
    t_convw = own_part(CONVC, CONVK).T
    t_convb = own_part(CONVC)[0]
    heads = small_total[place:].reshape(3, MH)
    return (
        result[None],
        d_hidden[None],
        jnp.concatenate([tot_c[:, :QKV], tot_m[:, 2 * D :], tot_c[:, QKV:]], 1),
        tot_mo,
        tot_fi,
        tot_fo,
        tg_in,
        tg_ff,
        tg_mix,
        t_convw,
        t_convb,
        heads[0],
        heads[1],
        heads[2],
    )


def solution(mesh):
    return jax.shard_map(
        body,
        mesh=mesh,
        in_specs=(
            P("fsdp", "ctx", None),
            P("fsdp", "ctx", None),
            P("fsdp", "ctx"),
            P("fsdp", None),
            P("fsdp", None),
            P("fsdp", None),
            P("fsdp", None),
            P("fsdp"),
            P("fsdp"),
            P("fsdp"),
            P("fsdp", None),
            P("fsdp"),
            P(),
            P(),
            P(),
        ),
        out_specs=(
            P("fsdp", "ctx", None),
            P("fsdp", "ctx", None),
            P("fsdp", None),
            P("fsdp", None),
            P("fsdp", None),
            P("fsdp", None),
            P("fsdp"),
            P("fsdp"),
            P("fsdp"),
            P("fsdp", None),
            P("fsdp"),
            P(),
            P(),
            P(),
        ),
        check_vma=False,
    )
```

```python
import functools
import math

import jax
import jax.numpy as jnp
from jax import lax
from jax.experimental import pallas as pl
from jax.experimental.pallas import tpu as pltpu
from jax.sharding import PartitionSpec as P

D = 1024
FF = 2048
NHQ = 8
NHKV = 2
HD = 64
MH = 24
MP = 64
NSTATE = 128
CONVK = 4
GQ = 4
ATTW = 512
KVW = 128
MDIM = 1536
CONVC = 1792
QKV = ATTW + 2 * KVW
NIN = 4120
PAIRS = MH // 2
PW = 2 * MP

EPS = 1e-05
FULL_PRECISION = lax.Precision.HIGHEST
F32 = jnp.float32
BF16 = jnp.bfloat16
VMEM_LIMIT = 48 * 1024 * 1024


def f32(value):
    return value.astype(F32)


def low(value):
    return value.astype(BF16)


def dot_mid(left, right):
    return lax.dot_general(left, right, (((1,), (0,)), ((), ())), preferred_element_type=F32)


def dot_last(left, right):
    return lax.dot_general(left, right, (((1,), (1,)), ((), ())), preferred_element_type=F32)


def dot_first(left, right):
    return lax.dot_general(left, right, (((0,), (0,)), ((), ())), preferred_element_type=F32)


def shifted(value, axis, steps):
    count = lax.axis_size(axis)
    initial, last = (max(0, -steps), min(count, count - steps))
    return lax.ppermute(value, axis, [(source, source + steps) for source in range(initial, last)])


def rope_tables(positions):
    inverse = 10000.0 ** (-2.0 * jnp.arange(HD // 2, dtype=F32) / HD)
    angles = positions.astype(F32)[:, None] * inverse[None, :]
    return (jnp.cos(angles), jnp.sin(angles))


def rotate_heads(shaped, cos_tab, sin_tab):
    first_half = shaped[..., : HD // 2]
    second = shaped[..., HD // 2 :]
    return jnp.concatenate(
        [first_half * cos_tab - second * sin_tab, second * cos_tab + first_half * sin_tab], -1
    )


def heads_first(flat):
    return flat.reshape(flat.shape[0], -1, HD).transpose(1, 0, 2)


def heads_flat(grouped):
    return grouped.transpose(1, 0, 2).reshape(grouped.shape[1], -1)


def att_scores(q_ref, k_ref, keydoc_ref, rowdoc_ref, keypos_ref, rowpos_ref):
    raw = dot_last(q_ref[0], k_ref[0]) * (1.0 / math.sqrt(HD))
    allowed = (keypos_ref[...] <= rowpos_ref[...]) & (keydoc_ref[...] == rowdoc_ref[...])
    return jnp.where(allowed, raw, -1e30)


def att_fwd_kernel(q_ref, k_ref, v_ref, keydoc_ref, rowdoc_ref, keypos_ref, rowpos_ref, o_ref, lse_ref):
    scores = att_scores(q_ref, k_ref, keydoc_ref, rowdoc_ref, keypos_ref, rowpos_ref)
    highest = jnp.max(scores, -1, keepdims=True)
    expo = jnp.exp(scores - highest)
    total = jnp.sum(expo, -1, keepdims=True)
    probs = low(expo * (1.0 / total))
    o_ref[0] = low(dot_mid(probs, v_ref[0]))
    lse_ref[0] = highest + jnp.log(total)


def att_bwd_kernel(
    q_ref, k_ref, v_ref, do_ref, lse_ref, keydoc_ref, rowdoc_ref, keypos_ref, rowpos_ref, *rest
):
    dq_ref, dk_ref, dv_ref = rest[-3:]
    head = pl.program_id(0)
    scores = att_scores(q_ref, k_ref, keydoc_ref, rowdoc_ref, keypos_ref, rowpos_ref)
    probs = jnp.exp(scores - lse_ref[0])
    d_out = do_ref[0]
    d_probs = dot_last(d_out, v_ref[0])
    centre = jnp.sum(probs * d_probs, -1, keepdims=True)
    d_scores = low(probs * (d_probs - centre))
    scale = 1.0 / math.sqrt(HD)
    dq_ref[0] = dot_mid(d_scores, k_ref[0]) * scale
    dk_term = dot_first(d_scores, q_ref[0]) * scale
    dv_term = dot_first(low(probs), d_out)

    @pl.when(head % GQ == 0)
    def _():
        dk_ref[0] = dk_term
        dv_ref[0] = dv_term

    @pl.when(head % GQ != 0)
    def _():
        dk_ref[0] += dk_term
        dv_ref[0] += dv_term


def unread(arrays):
    return [pl.BlockSpec(memory_space=pl.ANY)] * len(arrays)


def att_specs(rows, length):
    whole = lambda shape: pl.BlockSpec(shape, lambda h: (0, 0))
    per_q = pl.BlockSpec((1, rows, HD), lambda h: (h, 0, 0))
    per_kv = pl.BlockSpec((1, length, HD), lambda h: (h // GQ, 0, 0))
    lse = pl.BlockSpec((1, rows, 1), lambda h: (h, 0, 0))
    marks = [whole((1, length)), whole((rows, 1)), whole((1, length)), whole((rows, 1))]
    return per_q, per_kv, lse, marks


def att_cost(rows, length, dots):
    return pl.CostEstimate(
        flops=2 * dots * NHQ * rows * length * HD,
        transcendentals=NHQ * rows * length,
        bytes_accessed=4 * (NHQ * rows + NHKV * length) * HD * 2,
    )


def att_forward(q, k, v, key_doc, row_doc, key_pos, row_pos):
    rows, length = q.shape[1], k.shape[1]
    per_q, per_kv, lse, marks = att_specs(rows, length)
    return pl.pallas_call(
        att_fwd_kernel,
        name="attention_forward",
        grid=(NHQ,),
        in_specs=[per_q, per_kv, per_kv, *marks],
        out_specs=[per_q, lse],
        out_shape=[
            jax.ShapeDtypeStruct((NHQ, rows, HD), BF16),
            jax.ShapeDtypeStruct((NHQ, rows, 1), F32),
        ],
        cost_estimate=att_cost(rows, length, 2),
        compiler_params=pltpu.CompilerParams(vmem_limit_bytes=VMEM_LIMIT),
    )(q, k, v, key_doc, row_doc, key_pos, row_pos)


def att_backward(q, k, v, d_out, log_total, key_doc, row_doc, key_pos, row_pos, earlier):
    rows, length = q.shape[1], k.shape[1]
    per_q, per_kv, lse, marks = att_specs(rows, length)
    return pl.pallas_call(
        att_bwd_kernel,
        name="attention_backward",
        grid=(NHQ,),
        in_specs=[per_q, per_kv, per_kv, per_q, lse, *marks, *unread(earlier)],
        out_specs=[per_q, per_kv, per_kv],
        out_shape=[
            jax.ShapeDtypeStruct((NHQ, rows, HD), F32),
            jax.ShapeDtypeStruct((NHKV, length, HD), F32),
            jax.ShapeDtypeStruct((NHKV, length, HD), F32),
        ],
        cost_estimate=att_cost(rows, length, 5),
        compiler_params=pltpu.CompilerParams(vmem_limit_bytes=VMEM_LIMIT),
    )(q, k, v, d_out, log_total, key_doc, row_doc, key_pos, row_pos, *earlier)


def column_of(table, head):
    lanes = lax.broadcasted_iota(jnp.int32, table.shape, 1)
    return jnp.sum(jnp.where(lanes == head, table, 0.0), 1, keepdims=True)


def decay_matrix(cum_ref, cumt_ref, head):
    column = column_of(cum_ref[...], head)
    row = cumt_ref[pl.ds(head, 1), :]
    rows = column.shape[0]
    at = lax.broadcasted_iota(jnp.int32, (rows, rows), 0)
    source = lax.broadcasted_iota(jnp.int32, (rows, rows), 1)
    return column, row, jnp.exp(jnp.where(at >= source, column - row, -1e30))


def first_half_lanes(shape):
    return lax.broadcasted_iota(jnp.int32, shape, 1) < MP


def ssd_fwd_kernel(
    x_ref, b_ref, c_ref, dt_ref, cum_ref, dtt_ref, cumt_ref, y_ref, state_ref, inner
):
    pair = pl.program_id(0)
    b_in = low(b_ref[...])

    @pl.when(pair == 0)
    def _():
        inner[...] = dot_last(low(c_ref[...]), b_in)

    x_pair = x_ref[...]
    x_low = low(x_pair)
    parts, weights = [], []
    for i in range(2):
        head = 2 * pair + i
        column, row, decays = decay_matrix(cum_ref, cumt_ref, head)
        mixing = low(decays * inner[...] * dtt_ref[pl.ds(head, 1), :])
        parts.append(dot_mid(mixing, x_low))
        rows = column.shape[0]
        weights.append(jnp.exp(row[:, rows - 1 :] - column) * column_of(dt_ref[...], head))
    left = first_half_lanes(x_pair.shape)
    y_ref[...] = jnp.where(left, parts[0], parts[1])
    weighted = low(x_pair * jnp.where(left, weights[0], weights[1]))
    state_ref[...] = low(dot_first(weighted, b_in))


def ssd_bwd_kernel(
    x_ref, b_ref, c_ref, dy_ref, cum_ref, dtt_ref, cumt_ref, *rest
):
    dx_ref, db_ref, dc_ref, inner, d_inner = rest[-5:]
    pair = pl.program_id(0)
    b_in = low(b_ref[...])
    c_out = low(c_ref[...])

    @pl.when(pair == 0)
    def _():
        inner[...] = dot_last(c_out, b_in)
        d_inner[...] = jnp.zeros_like(d_inner)

    x_low = low(x_ref[...])
    dy_low = low(dy_ref[...])
    left = first_half_lanes(x_low.shape)
    parts = []
    for i in range(2):
        head = 2 * pair + i
        _, _, decays = decay_matrix(cum_ref, cumt_ref, head)
        scaled = decays * dtt_ref[pl.ds(head, 1), :]
        mixing = low(scaled * inner[...])
        parts.append(dot_first(mixing, dy_low))
        mine = left if i == 0 else jnp.logical_not(left)
        d_mixing = dot_last(jnp.where(mine, dy_low, jnp.zeros_like(dy_low)), x_low)
        d_inner[...] += d_mixing * scaled
    dx_ref[...] = jnp.where(left, parts[0], parts[1])

    @pl.when(pair == PAIRS - 1)
    def _():
        d_low = low(d_inner[...])
        dc_ref[...] = dot_mid(d_low, b_in)
        db_ref[...] = dot_first(d_low, c_out)


def ssd_join_kernel(
    x_ref, b_ref, dxl_ref, dy_ref, y_ref, state_ref, dstate_ref, dt_ref, cum_ref, cumt_ref,
    dbl_ref, dcl_ref, *rest,
):
    dx_ref, db_ref, dc_ref, row_ref, coll_ref, cols_ref, edge_ref = rest[-7:]
    pair = pl.program_id(0)
    x_pair = x_ref[...]
    left = first_half_lanes(x_pair.shape)
    rows = x_pair.shape[0]

    @pl.when(pair == 0)
    def _():
        db_ref[...] = dbl_ref[...]
        dc_ref[...] = dcl_ref[...]
        row_ref[...] = jnp.zeros_like(row_ref)
        coll_ref[...] = jnp.zeros_like(coll_ref)
        cols_ref[...] = jnp.zeros_like(cols_ref)
        edge_ref[...] = jnp.zeros_like(edge_ref)

    weights, growth, ends = [], [], []
    for i in range(2):
        head = 2 * pair + i
        column = column_of(cum_ref[...], head)
        end = cumt_ref[pl.ds(head, 1), :][:, rows - 1 :]
        weights.append(jnp.exp(end - column) * column_of(dt_ref[...], head))
        growth.append(jnp.exp(column))
        ends.append(jnp.exp(end))
    weight = jnp.where(left, weights[0], weights[1])
    grown = jnp.where(left, growth[0], growth[1])
    state = state_ref[...]
    d_state = dstate_ref[...]
    d_y = dy_ref[...]
    x_low = low(x_pair)
    weighted = low(x_pair * weight)
    through = dot_last(low(b_ref[...]), d_state)
    dx_ref[...] = dxl_ref[...] + weight * through
    db_ref[...] += dot_mid(weighted, d_state)
    dc_ref[...] += dot_mid(low(d_y * grown), state)
    row_term = f32(low(d_y)) * y_ref[...]
    local_term = f32(x_low) * dxl_ref[...]
    state_term = f32(weighted) * through
    met = f32(state) * f32(d_state)
    lanes = lax.broadcasted_iota(jnp.int32, row_ref.shape, 1)
    edge_lanes = lax.broadcasted_iota(jnp.int32, edge_ref.shape, 1)
    for i in range(2):
        mine = left if i == 0 else jnp.logical_not(left)
        here = lanes == 2 * pair + i
        for ref, term in ((row_ref, row_term), (coll_ref, local_term), (cols_ref, state_term)):
            total = jnp.sum(jnp.where(mine, term, 0.0), 1, keepdims=True)
            ref[...] = jnp.where(here, total, ref[...])
        half = met[i * MP : (i + 1) * MP]
        across = jnp.sum(jnp.sum(half, 1, keepdims=True), 0, keepdims=True) * ends[i]
        edge_ref[...] = jnp.where(edge_lanes == 2 * pair + i, across, edge_ref[...])


def ssd_cost(rows, dots, width):
    return pl.CostEstimate(
        flops=2 * dots * MH * rows * rows * PW,
        transcendentals=MH * rows * rows,
        bytes_accessed=4 * rows * MDIM * width,
    )


def ssd_specs(rows):
    pair_of = pl.BlockSpec((rows, PW), lambda p: (0, p))
    b_of = pl.BlockSpec((rows, NSTATE), lambda p: (0, PAIRS))
    c_of = pl.BlockSpec((rows, NSTATE), lambda p: (0, PAIRS + 1))
    once = pl.BlockSpec((rows, NSTATE), lambda p: (0, 0))
    tall = pl.BlockSpec((rows, MH), lambda p: (0, 0))
    wide = pl.BlockSpec((MH, rows), lambda p: (0, 0))
    state = pl.BlockSpec((PW, NSTATE), lambda p: (p, 0))
    return pair_of, b_of, c_of, once, tall, wide, state


def ssd_forward(act, dt_val, cum, dt_turned, cum_turned):
    rows = act.shape[0]
    pair_of, b_of, c_of, _, tall, wide, state = ssd_specs(rows)
    return pl.pallas_call(
        ssd_fwd_kernel,
        name="ssd_forward",
        grid=(PAIRS,),
        in_specs=[pair_of, b_of, c_of, tall, tall, wide, wide],
        out_specs=[pair_of, state],
        out_shape=[
            jax.ShapeDtypeStruct((rows, MDIM), F32),
            jax.ShapeDtypeStruct((MDIM, NSTATE), BF16),
        ],
        scratch_shapes=[pltpu.VMEM((rows, rows), F32)],
        cost_estimate=ssd_cost(rows, 1, 2),
        compiler_params=pltpu.CompilerParams(vmem_limit_bytes=VMEM_LIMIT),
    )(act, act, act, dt_val, cum, dt_turned, cum_turned)


def ssd_backward(act, d_y, cum, dt_turned, cum_turned, earlier):
    rows = act.shape[0]
    pair_of, b_of, c_of, once, tall, wide, _ = ssd_specs(rows)
    return pl.pallas_call(
        ssd_bwd_kernel,
        name="ssd_backward",
        grid=(PAIRS,),
        in_specs=[pair_of, b_of, c_of, pair_of, tall, wide, wide, *unread(earlier)],
        out_specs=[pair_of, once, once],
        out_shape=[
            jax.ShapeDtypeStruct((rows, MDIM), F32),
            jax.ShapeDtypeStruct((rows, NSTATE), F32),
            jax.ShapeDtypeStruct((rows, NSTATE), F32),
        ],
        scratch_shapes=[pltpu.VMEM((rows, rows), F32), pltpu.VMEM((rows, rows), F32)],
        cost_estimate=ssd_cost(rows, 2, 3),
        compiler_params=pltpu.CompilerParams(vmem_limit_bytes=VMEM_LIMIT),
    )(act, act, act, d_y, cum, dt_turned, cum_turned, *earlier)


def ssd_join(
    act, dx_local, d_y, y_ssd, state, d_state, dt_val, cum, cum_turned, db_local, dc_local, earlier
):
    rows = act.shape[0]
    pair_of, b_of, _, once, tall, wide, state_of = ssd_specs(rows)
    edge = pl.BlockSpec((1, MH), lambda p: (0, 0))
    return pl.pallas_call(
        ssd_join_kernel,
        name="ssd_join",
        grid=(PAIRS,),
        in_specs=[
            pair_of, b_of, pair_of, pair_of, pair_of, state_of, state_of, tall, tall, wide,
            once, once, *unread(earlier),
        ],
        out_specs=[pair_of, once, once, tall, tall, tall, edge],
        out_shape=[
            jax.ShapeDtypeStruct((rows, MDIM), F32),
            jax.ShapeDtypeStruct((rows, NSTATE), F32),
            jax.ShapeDtypeStruct((rows, NSTATE), F32),
            jax.ShapeDtypeStruct((rows, MH), F32),
            jax.ShapeDtypeStruct((rows, MH), F32),
            jax.ShapeDtypeStruct((rows, MH), F32),
            jax.ShapeDtypeStruct((1, MH), F32),
        ],
        cost_estimate=pl.CostEstimate(
            flops=6 * rows * MDIM * NSTATE,
            transcendentals=3 * rows * MH,
            bytes_accessed=4 * rows * MDIM * 5,
        ),
        compiler_params=pltpu.CompilerParams(vmem_limit_bytes=VMEM_LIMIT),
    )(
        act, act, dx_local, d_y, y_ssd, state, d_state, dt_val, cum, cum_turned, db_local, dc_local,
        *earlier,
    )


STEPS = 4


def square_of(ref):
    block = ref[...]
    return block.reshape(block.shape[0] * block.shape[1], block.shape[2])


def call_ffn(kernel, name, in_specs, out_specs, out_shape, flops, operands, scratch=()):
    return pl.pallas_call(
        kernel,
        name=name,
        grid=(STEPS,),
        in_specs=in_specs,
        out_specs=out_specs,
        out_shape=out_shape,
        scratch_shapes=list(scratch),
        cost_estimate=pl.CostEstimate(flops=flops, transcendentals=0, bytes_accessed=flops // 256),
        compiler_params=pltpu.CompilerParams(vmem_limit_bytes=VMEM_LIMIT),
    )(*operands)


def whole_of(shape):
    return pl.BlockSpec(shape, lambda k: (0,) * len(shape))


def column_block(rows, width):
    return pl.BlockSpec((rows, width), lambda k: (0, k))


def devices_block(stack, part):
    count, tall, _ = stack.shape
    return pl.BlockSpec((count // STEPS, tall // 4, D), lambda k: (k, part, 0))


def middle_kernel(hidden_ref, joined_ref, w_ref, gain_ref, middle_ref, ff_ref, scale_ref):
    step = pl.program_id(0)
    term = dot_mid(joined_ref[...], square_of(w_ref))

    @pl.when(step == 0)
    def _():
        middle_ref[...] = f32(hidden_ref[...]) + term

    @pl.when(step != 0)
    def _():
        middle_ref[...] += term

    @pl.when(step == STEPS - 1)
    def _():
        middle = middle_ref[...]
        scale = lax.rsqrt(jnp.mean(middle * middle, -1, keepdims=True) + EPS)
        scale_ref[...] = scale
        ff_ref[...] = low(middle * scale * gain_ref[...])


def ffn_middle(hidden, joined, stack, gain):
    rows, width = joined.shape
    return call_ffn(
        middle_kernel,
        "middle",
        [
            whole_of((rows, D)),
            column_block(rows, width // STEPS),
            devices_block(stack, 2),
            whole_of((1, D)),
        ],
        [whole_of((rows, D)), whole_of((rows, D)), whole_of((rows, 1))],
        [
            jax.ShapeDtypeStruct((rows, D), F32),
            jax.ShapeDtypeStruct((rows, D), BF16),
            jax.ShapeDtypeStruct((rows, 1), F32),
        ],
        2 * rows * width * D,
        (hidden, joined, stack, gain),
    )


def gate_kernel(ff_ref, gate_w_ref, up_w_ref, gate_ref, up_ref, act_ref):
    ff = ff_ref[...]
    gate = dot_mid(ff, square_of(gate_w_ref))
    up = dot_mid(ff, square_of(up_w_ref))
    gate_ref[...] = gate
    up_ref[...] = up
    act_ref[...] = low(gate * jax.nn.sigmoid(gate) * up)


def ffn_gate(ff, stack):
    rows = ff.shape[0]
    count, tall, _ = stack.shape
    quarter = lambda first: pl.BlockSpec(
        (count, tall // 8, D // 2), lambda k: (0, first + k // 2, k % 2)
    )
    out = column_block(rows, FF // STEPS)
    return call_ffn(
        gate_kernel,
        "gate_up",
        [whole_of((rows, D)), quarter(0), quarter(2)],
        [out, out, out],
        [
            jax.ShapeDtypeStruct((rows, FF), F32),
            jax.ShapeDtypeStruct((rows, FF), F32),
            jax.ShapeDtypeStruct((rows, FF), BF16),
        ],
        4 * rows * FF * D,
        (ff, stack, stack),
    )


def output_kernel(middle_ref, act_ref, w_ref, *rest):
    out_ref, total = rest[-2:]
    step = pl.program_id(0)
    term = dot_mid(act_ref[...], square_of(w_ref))

    @pl.when(step == 0)
    def _():
        total[...] = middle_ref[...] + term

    @pl.when(step != 0)
    def _():
        total[...] += term

    @pl.when(step == STEPS - 1)
    def _():
        out_ref[...] = low(total[...])


def ffn_output(middle, act, stack, earlier):
    rows, width = act.shape
    return call_ffn(
        output_kernel,
        "layer_output",
        [
            whole_of((rows, D)),
            column_block(rows, width // STEPS),
            devices_block(stack, 3),
            *unread(earlier),
        ],
        whole_of((rows, D)),
        jax.ShapeDtypeStruct((rows, D), BF16),
        2 * rows * width * D,
        (middle, act, stack, *earlier),
        [pltpu.VMEM((rows, D), F32)],
    )


def d_gate_kernel(cot_ref, w_ref, gate_ref, up_ref, *rest):
    d_ref = rest[-1]
    step = pl.program_id(0)
    width = gate_ref.shape[1]
    d_act = dot_last(cot_ref[...], square_of(w_ref))
    gate = gate_ref[...]
    sigma = jax.nn.sigmoid(gate)
    start = pl.multiple_of(step * width, 128)
    d_ref[:, pl.ds(start, width)] = low(d_act * up_ref[...] * silu_slope(gate, sigma))
    d_ref[:, pl.ds(start + FF, width)] = low(d_act * (gate * sigma))


def ffn_d_gate(cot, stack, gate, up, earlier):
    rows = cot.shape[0]
    block = column_block(rows, FF // STEPS)
    return call_ffn(
        d_gate_kernel,
        "d_gate_up",
        [whole_of((rows, D)), devices_block(stack, 3), block, block, *unread(earlier)],
        whole_of((rows, 2 * FF)),
        jax.ShapeDtypeStruct((rows, 2 * FF), BF16),
        2 * rows * FF * D,
        (cot, stack, gate, up, *earlier),
    )


def d_middle_kernel(d_gu_ref, w_ref, middle_ref, scale_ref, gain_ref, cot_ref, *rest):
    d_ref, low_ref, gain_grad_ref = rest[-3:]
    step = pl.program_id(0)
    term = dot_last(d_gu_ref[...], square_of(w_ref))

    @pl.when(step == 0)
    def _():
        d_ref[...] = term

    @pl.when(step != 0)
    def _():
        d_ref[...] += term

    @pl.when(step == STEPS - 1)
    def _():
        d_normed = d_ref[...]
        scale = scale_ref[...]
        unit = middle_ref[...] * scale
        gain_grad_ref[...] = jnp.sum(d_normed * unit, 0, keepdims=True)
        d_unit = d_normed * gain_ref[...]
        inner = jnp.mean(d_unit * unit, -1, keepdims=True)
        d_middle = f32(cot_ref[...]) + scale * (d_unit - unit * inner)
        d_ref[...] = d_middle
        low_ref[...] = low(d_middle)


def ffn_d_middle(d_gu, stack, middle, scale, gain, cot, earlier):
    rows = d_gu.shape[0]
    count, tall, _ = stack.shape
    whole = whole_of((rows, D))
    return call_ffn(
        d_middle_kernel,
        "d_middle",
        [
            column_block(rows, D),
            pl.BlockSpec((count, tall // 8, D), lambda k: (0, k, 0)),
            whole,
            whole_of((rows, 1)),
            whole_of((1, D)),
            whole,
            *unread(earlier),
        ],
        [whole, whole, whole_of((1, D))],
        [
            jax.ShapeDtypeStruct((rows, D), F32),
            jax.ShapeDtypeStruct((rows, D), BF16),
            jax.ShapeDtypeStruct((1, D), F32),
        ],
        4 * rows * FF * D,
        (d_gu, stack, middle, scale, gain, cot, *earlier),
    )


def d_joined_kernel(d_ref, w_ref, out_ref):
    out_ref[...] = low(dot_last(d_ref[...], square_of(w_ref)))


def mixer_d_joined(d_middle, stack):
    rows = d_middle.shape[0]
    width = 2 * D
    return call_ffn(
        d_joined_kernel,
        "d_joined",
        [whole_of((rows, D)), devices_block(stack, 2)],
        column_block(rows, width // STEPS),
        jax.ShapeDtypeStruct((rows, width), BF16),
        2 * rows * width * D,
        (d_middle, stack),
    )


def flipped(value, bit):
    count = lax.axis_size("fsdp")
    return lax.ppermute(value, "fsdp", [(i, i ^ bit) for i in range(count)])


def squares():
    return lax.axis_size("fsdp") == 8


def gather_rows(shard):
    return lax.all_gather(shard, "fsdp", axis=0, tiled=True)


def device_columns(left, flips, depth, offset):
    count = lax.axis_size("fsdp")
    stride = left.shape[1] // count
    me = lax.axis_index("fsdp")
    return jnp.concatenate(
        [
            lax.dynamic_slice_in_dim(left, (me ^ flip) * stride + offset, depth, 1)
            for flip in flips
        ],
        1,
    )


def products_kernel(left_ref, right_ref, *rest):
    out_ref = rest[-1]
    term = dot_first(left_ref[0], right_ref[...]).reshape(out_ref.shape)
    if len(rest) > 1:
        term = term + f32(rest[0][...])
    out_ref[...] = low(term)


def products(lefts, right, group, came=()):
    rows, columns = right.shape
    depth, step = group.depth, group.step
    out = pl.BlockSpec((4, depth, step), lambda k: (0, 0, k))
    return pl.pallas_call(
        products_kernel,
        name="gradient_rows",
        grid=(columns // step,),
        in_specs=[
            pl.BlockSpec((1, rows, 4 * depth), lambda k: (group.left_of(k), 0, 0)),
            pl.BlockSpec((rows, step), lambda k: (0, k)),
            *([out] * len(came)),
        ],
        out_specs=out,
        out_shape=jax.ShapeDtypeStruct((4, depth, columns), BF16),
        cost_estimate=pl.CostEstimate(
            flops=8 * rows * depth * columns,
            transcendentals=0,
            bytes_accessed=8 * depth * columns * (1 + len(came)),
        ),
        compiler_params=pltpu.CompilerParams(vmem_limit_bytes=VMEM_LIMIT),
    )(lefts, right, *came)


class Group:
    def __init__(self, lefts, counts, depth, step, left_of):
        self.counts, self.depth, self.step, self.left_of = counts, depth, step, left_of
        self.lefts = lefts
        if squares():
            self.theirs, self.mine = [
                jnp.stack([device_columns(left, flips, depth, at) for left, at in lefts])
                for flips in ((1, 3, 5, 7), (0, 2, 4, 6))
            ]


def scatter_open(group, right):
    if squares():
        return products(group.theirs, right, group)
    count = lax.axis_size("fsdp")
    whole, first = [], 0
    for (left, at), columns in zip(group.lefts, group.counts):
        rows = left.reshape(left.shape[0], count, -1)[:, :, at : at + group.depth]
        part = right[:, first : first + columns]
        whole.append(low(dot_first(rows.reshape(left.shape[0], -1), part)))
        first += columns
    return lax.psum_scatter(
        jnp.concatenate(whole, 1), "fsdp", scatter_dimension=0, tiled=True
    )


def scatter_swap(group, right, theirs):
    if not squares():
        return theirs
    return products(group.mine, right, group, [flipped(theirs, 1)])


def scatter_first(ours):
    if not squares():
        return ours, ours
    half = ours.shape[1] // 2
    for_y = flipped(ours[3, :half], 2)
    for_x = flipped(ours[3, half:], 4)
    to_x = jnp.concatenate([ours[1, :half], low(f32(ours[1, half:]) + f32(for_x))], 0)
    to_y = jnp.concatenate([low(f32(ours[2, :half]) + f32(for_y)), ours[2, half:]], 0)
    return to_x, to_y


def scatter_last(ours, to_x, to_y):
    if not squares():
        return ours
    return low(f32(ours[0]) + f32(flipped(to_x, 2)) + f32(flipped(to_y, 4)))


def grid_total(value):
    if not squares() or lax.axis_size("ctx") != 4:
        return lax.psum(value, ("ctx", "fsdp"))
    for bit in (1, 2, 4):
        value = value + flipped(value, bit)
    for bit in (1, 2):
        value = value + ctx_flipped(value, bit)
    return value


def ctx_flipped(value, bit):
    return lax.ppermute(value, "ctx", [(i, i ^ bit) for i in range(lax.axis_size("ctx"))])


def ctx_total(part, earlier=()):
    if lax.axis_size("ctx") != 4:
        return f32(lax.psum(part, "ctx"))
    me = lax.axis_index("ctx")
    value = part
    for bit in (1, 2):
        size = value.shape[0] // 2
        upper = (me // bit) % 2
        mine = lax.dynamic_slice_in_dim(value, upper * size, size, 0)
        theirs = lax.dynamic_slice_in_dim(value, (1 - upper) * size, size, 0)
        value = low(f32(mine) + f32(ctx_flipped(theirs, bit)))
    value = after(value, earlier)
    for bit in (2, 1):
        upper = (me // bit) % 2
        other = ctx_flipped(value, bit)
        value = jnp.concatenate(
            [jnp.where(upper == 0, value, other), jnp.where(upper == 0, other, value)], 0
        )
    return f32(value)


def entering(own, decay, direction):
    count = lax.axis_size("ctx")
    coarse = low(decay)
    fine = low(decay - f32(coarse))
    line = jnp.concatenate([coarse, fine, jnp.zeros((NSTATE - 2 * MH,), BF16)])
    packed = jnp.concatenate([own, jnp.broadcast_to(line[None], (16, NSTATE))], 0)
    total = jnp.zeros(own.shape, F32)
    carried = jnp.ones(decay.shape, F32)
    for distance in range(1, count):
        came = shifted(packed, "ctx", direction * distance)
        total = total + f32(came[:MDIM]) * jnp.repeat(carried, MP)[:, None]
        line = f32(came[MDIM])
        carried = carried * (line[:MH] + line[MH : 2 * MH])
    return total


def after(value, earlier):
    return lax.optimization_barrier((value, earlier))[0]


def silu_slope(value, sigma):
    return sigma * (1.0 + value * (1.0 - sigma))


def body(
    hidden,
    cotangent,
    doc_ids,
    mixer_in_weight,
    mixer_out_weight,
    feedforward_in_weight,
    feedforward_out_weight,
    gain_in,
    gain_ff,
    gain_mix,
    conv_weight,
    conv_bias,
    dt_bias,
    a_log,
    d_skip,
):
    rows = hidden.shape[1]
    shards = lax.axis_size("fsdp")

    small = [gain_in, gain_ff, gain_mix, conv_weight.T.reshape(-1), conv_bias]
    sizes = [piece.shape[0] for piece in small]
    depth = mixer_in_weight.shape[0]
    width_cd = NIN - QKV - MDIM
    lines = -(-sum(sizes) // depth)
    line = jnp.concatenate(small + [jnp.zeros((lines * depth - sum(sizes),), BF16)])
    full_in = gather_rows(
        jnp.concatenate([mixer_in_weight, line.reshape(lines, depth).T], 1)
    )
    full_qkv = full_in[:, :QKV]
    full_z = full_in[:, QKV : QKV + MDIM]
    full_cd = full_in[:, QKV + MDIM : NIN]

    small_all = f32(full_in[:, NIN:]).T.reshape(lines, shards, depth)
    small_all = small_all.transpose(1, 0, 2).reshape(shards, lines * depth)
    cuts = [sum(sizes[:i]) for i in range(len(sizes) + 1)]
    gin, gff, gmix, convw, convb = [
        small_all[:, cuts[i] : cuts[i + 1]] for i in range(len(sizes))
    ]
    gin, gff, gmix, convb = [piece.reshape(-1) for piece in (gin, gff, gmix, convb)]
    convw = convw.reshape(shards, CONVK, -1).transpose(1, 0, 2).reshape(CONVK, CONVC)

    quarters = [feedforward_in_weight[:, i * D : (i + 1) * D] for i in range(4)]
    stack = lax.all_gather(
        jnp.concatenate([*quarters, mixer_out_weight, feedforward_out_weight], 0), "fsdp", axis=0
    )

    hidden32 = f32(hidden[0])
    scale_in = lax.rsqrt(jnp.mean(hidden32 * hidden32, -1, keepdims=True) + EPS)
    normed_b = low(hidden32 * scale_in * gin)

    proj_cd = dot_mid(normed_b, full_cd)
    conv_in = proj_cd[:, :CONVC]
    dt_raw = proj_cd[:, CONVC:]
    rim = shifted(conv_in[rows - (CONVK - 1) :], "ctx", 1)
    extended = jnp.concatenate([rim, conv_in], 0)
    u = convb
    for tap in range(CONVK):
        u = u + convw[tap] * extended[tap : tap + rows]
    u_sigma = jax.nn.sigmoid(u)
    act = u * u_sigma
    dt_arg = dt_raw + dt_bias
    dt_val = jax.nn.softplus(dt_arg)
    rate = -jnp.exp(a_log)
    log_decay = rate * dt_val
    ones = (jnp.arange(rows)[:, None] >= jnp.arange(rows)[None, :]).astype(F32)
    cum = lax.dot_general(ones, log_decay, (((1,), (0,)), ((), ())), precision=FULL_PRECISION)
    cum_turned = cum.T
    dt_turned = dt_val.T
    y_local, own_state = ssd_forward(act, dt_val, cum, dt_turned, cum_turned)
    own_decay = jnp.exp(cum[-1])

    proj_qkv = dot_mid(normed_b, full_qkv)
    positions = lax.axis_index("ctx") * rows + jnp.arange(rows)
    cos_tab, sin_tab = rope_tables(positions)
    q_heads = low(rotate_heads(heads_first(proj_qkv[:, :ATTW]), cos_tab, sin_tab))
    k_heads = low(rotate_heads(heads_first(proj_qkv[:, ATTW : ATTW + KVW]), cos_tab, sin_tab))
    v_heads = low(heads_first(proj_qkv[:, ATTW + KVW :]))
    doc_here = low(doc_ids[0])
    doc_line = jnp.concatenate([doc_here, jnp.zeros((2 * KVW - rows,), BF16)])
    own_kv = jnp.concatenate(
        [
            jnp.concatenate([heads_flat(k_heads), heads_flat(v_heads)], 1),
            jnp.broadcast_to(doc_line[None], (16, 2 * KVW)),
        ],
        0,
    )
    blocks = lax.axis_size("ctx")
    me = lax.axis_index("ctx")
    came = [own_kv] + [shifted(own_kv, "ctx", distance) for distance in range(1, blocks)]
    kv_all = jnp.concatenate([block[:rows] for block in came], 0)
    k_all = heads_first(kv_all[:, :KVW])
    v_all = heads_first(kv_all[:, KVW:])
    key_doc = jnp.concatenate([block[rows, :rows] for block in came])[None, :].astype(jnp.int32)
    row_doc = doc_ids[0][:, None]
    row_pos = positions.astype(jnp.int32)[:, None]
    key_pos = jnp.concatenate(
        [
            jnp.where(me >= distance, positions - distance * rows, blocks * rows)
            for distance in range(blocks)
        ]
    )[None, :]
    attended, log_total = att_forward(q_heads, k_all, v_all, key_doc, row_doc, key_pos, row_pos)

    state_in = low(entering(own_state, own_decay, 1))
    spread = (jnp.arange(MH)[:, None] == (jnp.arange(MDIM) // MP)[None, :]).astype(F32)
    grown = lax.dot_general(
        jnp.exp(cum), spread, (((1,), (0,)), ((), ())), precision=FULL_PRECISION
    )
    x_flat = act[:, :MDIM]
    c_low = low(act[:, MDIM + NSTATE :])
    y_ssd = y_local + grown * dot_last(c_low, state_in)
    z_gate = dot_mid(normed_b, full_z)
    skip = jnp.repeat(d_skip, MP)
    y_full = y_ssd + skip * x_flat
    z_sigma = jax.nn.sigmoid(z_gate)
    z_act = z_gate * z_sigma
    gated = y_full * z_act
    scale_mix = lax.rsqrt(jnp.mean(gated * gated, -1, keepdims=True) + EPS)
    joined_b = jnp.concatenate(
        [heads_flat(attended), low(gated * scale_mix * gmix)], 1
    )

    cot_b = cotangent[0]
    middle, ff_b, scale_ff = ffn_middle(hidden[0], joined_b, stack, gff[None])
    gate_val, up_val, act_b = ffn_gate(ff_b, stack)

    grad_fo = low(dot_first(act_b, cot_b))
    part_fo = lax.psum_scatter(grad_fo, "fsdp", scatter_dimension=0, tiled=True)
    d_gu = ffn_d_gate(cot_b, stack, gate_val, up_val, [grad_fo])
    grad_fi = low(dot_first(ff_b, d_gu))
    part_fi = lax.psum_scatter(grad_fi, "fsdp", scatter_dimension=0, tiled=True)
    d_middle, d_middle_b, dg_ff = ffn_d_middle(
        d_gu, stack, middle, scale_ff, gff[None], cot_b, [grad_fi]
    )
    dg_ff = dg_ff[0]
    d_joined = mixer_d_joined(d_middle_b, stack)
    d_mamba = f32(d_joined[:, ATTW:])
    unit_mix = gated * scale_mix
    dg_mix = jnp.sum(d_mamba * unit_mix, 0)
    d_unit_mix = d_mamba * gmix
    d_gated = scale_mix * (
        d_unit_mix - unit_mix * jnp.mean(d_unit_mix * unit_mix, -1, keepdims=True)
    )
    d_y = d_gated * z_act
    d_z = low(d_gated * y_full * silu_slope(z_gate, z_sigma))
    dd_skip = jnp.sum(jnp.sum(d_y * x_flat, 0).reshape(MH, MP), 1)
    local_grad = low(dot_first(low(d_y * grown), c_low))

    group_m = Group(
        [(joined_b, 0), (joined_b, depth), (normed_b, 0)],
        [D, D, MDIM],
        depth,
        D // 2,
        lambda k: jnp.minimum(k // 2, 2),
    )
    right_m = jnp.concatenate([d_middle_b, d_middle_b, d_z], 1)
    theirs_m = scatter_open(group_m, right_m)

    dx_local, db_local, dc_local = ssd_backward(
        act, d_y, cum, dt_turned, cum_turned, [local_grad]
    )
    d_state = low(entering(local_grad, own_decay, -1))
    do_heads = heads_first(d_joined[:, :ATTW])
    d_q, d_k, d_v = att_backward(
        q_heads, k_all, v_all, do_heads, log_total, key_doc, row_doc, key_pos, row_pos,
        [dx_local],
    )
    result = ffn_output(middle, act_b, stack, [d_q])
    d_kv = jnp.concatenate([heads_flat(d_k), heads_flat(d_v)], 1)
    terms = low(d_kv[rows:])
    terms = after(terms, (d_state, result))
    dx_ssd, d_b, d_c, row_term, col_local, col_state, edge = ssd_join(
        act, dx_local, d_y, y_ssd, state_in, d_state, dt_val, cum, cum_turned, db_local, dc_local,
        [theirs_m, part_fo, terms],
    )
    received = [
        shifted(terms[(distance - 1) * rows : distance * rows], "ctx", -distance)
        for distance in range(1, blocks)
    ]
    received, dx_ssd = lax.optimization_barrier((received, dx_ssd))
    dkv = d_kv[:rows] + sum(f32(term) for term in received)
    d_q = rotate_heads(d_q, cos_tab, -sin_tab)
    d_k = rotate_heads(heads_first(dkv[:, :KVW]), cos_tab, -sin_tab)
    d_qkv = jnp.concatenate([low(heads_flat(d_q)), low(heads_flat(d_k)), low(dkv[:, KVW:])], 1)
    col_term = col_local + col_state
    d_cum = row_term - col_term
    d_end = jnp.sum(col_state, 0) + edge[0]
    d_decay = (
        lax.dot_general(ones, d_cum, (((0,), (0,)), ((), ())), precision=FULL_PRECISION) + d_end
    )
    d_alog = jnp.sum(d_decay * log_decay, 0)
    dt_sigma = jax.nn.sigmoid(dt_arg)
    ratio = jnp.where(dt_arg < -30.0, 1.0, dt_sigma / jnp.where(dt_arg < -30.0, 1.0, dt_val))
    d_dtraw = col_term * ratio + d_decay * rate * dt_sigma
    d_dtbias = jnp.sum(d_dtraw, 0)

    d_act_conv = jnp.concatenate([dx_ssd + skip * d_y, d_b, d_c], 1)
    d_u = d_act_conv * silu_slope(u, u_sigma)
    d_convb = jnp.sum(d_u, 0)
    d_convw = jnp.stack(
        [jnp.sum(d_u * extended[tap : tap + rows], 0) for tap in range(CONVK)]
    )
    d_u_ext = jnp.concatenate([d_u, shifted(d_u[: CONVK - 1], "ctx", -1)], 0)
    d_conv_in = sum(
        convw[tap] * d_u_ext[CONVK - 1 - tap : CONVK - 1 - tap + rows] for tap in range(CONVK)
    )
    d_cd = jnp.concatenate([low(d_conv_in), low(d_dtraw)], 1)
    d_cd = after(d_cd, part_fi)
    lone = jnp.zeros((rows, -(QKV + width_cd) % 384), BF16)
    right_c = jnp.concatenate([d_qkv, d_cd, lone], 1)
    group_c = Group([(normed_b, 0)], [right_c.shape[1]], depth, 384, lambda k: 0)
    theirs_c = scatter_open(group_c, right_c)
    ours_m = scatter_swap(group_m, right_m, after(theirs_m, theirs_c))
    to_x_m, to_y_m = scatter_first(ours_m)
    ours_c = scatter_swap(group_c, right_c, theirs_c)
    ours_c = after(ours_c, (to_x_m, to_y_m))
    to_x_c, to_y_c = scatter_first(ours_c)
    part_m = scatter_last(ours_m, to_x_m, to_y_m)
    part_c = scatter_last(ours_c, to_x_c, to_y_c)

    d_normed = dot_last(d_cd, full_cd) + dot_last(d_qkv, full_qkv) + dot_last(d_z, full_z)
    unit_in = hidden32 * scale_in
    dg_in = jnp.sum(d_normed * unit_in, 0)
    d_unit_in = d_normed * gin
    d_hidden = d_middle + scale_in * (
        d_unit_in - unit_in * jnp.mean(d_unit_in * unit_in, -1, keepdims=True)
    )

    tot_f = lax.psum((part_fo, part_fi), "ctx")
    tot_f, parts = lax.optimization_barrier((tot_f, (part_m, part_c)))
    tot_m, tot_c = [f32(total) for total in lax.psum(parts, "ctx")]
    tot_fo, tot_fi = [f32(total) for total in tot_f]
    tot_mo = jnp.concatenate([tot_m[:, :D], tot_m[:, D : 2 * D]], 0)
    small_grads = jnp.concatenate(
        [dg_in, dg_ff, dg_mix, d_convw.reshape(-1), d_convb, d_dtbias, d_alog, dd_skip]
    )
    small_total = grid_total(small_grads)
    mine = lax.axis_index("fsdp")
    place = 0

    def own_part(width, count=1):
        nonlocal place
        block = small_total[place : place + width * count].reshape(count, width)
        place += width * count
        return lax.dynamic_slice_in_dim(block, mine * (width // shards), width // shards, 1)

    tg_in = own_part(D)[0]
    tg_ff = own_part(D)[0]
    tg_mix = own_part(MDIM)[0]
    t_convw = own_part(CONVC, CONVK).T
    t_convb = own_part(CONVC)[0]
    heads = small_total[place:].reshape(3, MH)
    return (
        result[None],
        d_hidden[None],
        jnp.concatenate([tot_c[:, :QKV], tot_m[:, 2 * D :], tot_c[:, QKV : QKV + width_cd]], 1),
        tot_mo,
        tot_fi,
        tot_fo,
        tg_in,
        tg_ff,
        tg_mix,
        t_convw,
        t_convb,
        heads[0],
        heads[1],
        heads[2],
    )


def solution(mesh):
    return jax.shard_map(
        body,
        mesh=mesh,
        in_specs=(
            P("fsdp", "ctx", None),
            P("fsdp", "ctx", None),
            P("fsdp", "ctx"),
            P("fsdp", None),
            P("fsdp", None),
            P("fsdp", None),
            P("fsdp", None),
            P("fsdp"),
            P("fsdp"),
            P("fsdp"),
            P("fsdp", None),
            P("fsdp"),
            P(),
            P(),
            P(),
        ),
        out_specs=(
            P("fsdp", "ctx", None),
            P("fsdp", "ctx", None),
            P("fsdp", None),
            P("fsdp", None),
            P("fsdp", None),
            P("fsdp", None),
            P("fsdp"),
            P("fsdp"),
            P("fsdp"),
            P("fsdp", None),
            P("fsdp"),
            P(),
            P(),
            P(),
        ),
        check_vma=False,
    )
```

```python
import functools
import math

import jax
import jax.numpy as jnp
from jax import lax
from jax.experimental import pallas as pl
from jax.experimental.pallas import tpu as pltpu
from jax.sharding import PartitionSpec as P

D = 1024
FF = 2048
NHQ = 8
NHKV = 2
HD = 64
MH = 24
MP = 64
NSTATE = 128
CONVK = 4
GQ = 4
ATTW = 512
KVW = 128
MDIM = 1536
CONVC = 1792
QKV = ATTW + 2 * KVW
NIN = 4120
PAIRS = MH // 2
PW = 2 * MP

EPS = 1e-05
FULL_PRECISION = lax.Precision.HIGHEST
F32 = jnp.float32
BF16 = jnp.bfloat16
VMEM_LIMIT = 48 * 1024 * 1024


def f32(value):
    return value.astype(F32)


def low(value):
    return value.astype(BF16)


def dot_mid(left, right):
    return lax.dot_general(left, right, (((1,), (0,)), ((), ())), preferred_element_type=F32)


def dot_last(left, right):
    return lax.dot_general(left, right, (((1,), (1,)), ((), ())), preferred_element_type=F32)


def dot_first(left, right):
    return lax.dot_general(left, right, (((0,), (0,)), ((), ())), preferred_element_type=F32)


def shifted(value, axis, steps):
    count = lax.axis_size(axis)
    initial, last = (max(0, -steps), min(count, count - steps))
    return lax.ppermute(value, axis, [(source, source + steps) for source in range(initial, last)])


def rope_tables(positions):
    inverse = 10000.0 ** (-2.0 * jnp.arange(HD // 2, dtype=F32) / HD)
    angles = positions.astype(F32)[:, None] * inverse[None, :]
    return (jnp.cos(angles), jnp.sin(angles))


def rotate_heads(shaped, cos_tab, sin_tab):
    first_half = shaped[..., : HD // 2]
    second = shaped[..., HD // 2 :]
    return jnp.concatenate(
        [first_half * cos_tab - second * sin_tab, second * cos_tab + first_half * sin_tab], -1
    )


def heads_first(flat):
    return flat.reshape(flat.shape[0], -1, HD).transpose(1, 0, 2)


def heads_flat(grouped):
    return grouped.transpose(1, 0, 2).reshape(grouped.shape[1], -1)


def att_scores(q_ref, k_ref, keydoc_ref, rowdoc_ref, keypos_ref, rowpos_ref):
    raw = dot_last(q_ref[0], k_ref[0]) * (1.0 / math.sqrt(HD))
    allowed = (keypos_ref[...] <= rowpos_ref[...]) & (keydoc_ref[...] == rowdoc_ref[...])
    return jnp.where(allowed, raw, -1e30)


def att_fwd_kernel(q_ref, k_ref, v_ref, keydoc_ref, rowdoc_ref, keypos_ref, rowpos_ref, o_ref, lse_ref):
    scores = att_scores(q_ref, k_ref, keydoc_ref, rowdoc_ref, keypos_ref, rowpos_ref)
    highest = jnp.max(scores, -1, keepdims=True)
    expo = jnp.exp(scores - highest)
    total = jnp.sum(expo, -1, keepdims=True)
    probs = low(expo * (1.0 / total))
    o_ref[0] = low(dot_mid(probs, v_ref[0]))
    lse_ref[0] = highest + jnp.log(total)


def att_bwd_kernel(
    q_ref, k_ref, v_ref, do_ref, lse_ref, keydoc_ref, rowdoc_ref, keypos_ref, rowpos_ref, *rest
):
    dq_ref, dk_ref, dv_ref = rest[-3:]
    head = pl.program_id(0)
    scores = att_scores(q_ref, k_ref, keydoc_ref, rowdoc_ref, keypos_ref, rowpos_ref)
    probs = jnp.exp(scores - lse_ref[0])
    d_out = do_ref[0]
    d_probs = dot_last(d_out, v_ref[0])
    centre = jnp.sum(probs * d_probs, -1, keepdims=True)
    d_scores = low(probs * (d_probs - centre))
    scale = 1.0 / math.sqrt(HD)
    dq_ref[0] = dot_mid(d_scores, k_ref[0]) * scale
    dk_term = dot_first(d_scores, q_ref[0]) * scale
    dv_term = dot_first(low(probs), d_out)

    @pl.when(head % GQ == 0)
    def _():
        dk_ref[0] = dk_term
        dv_ref[0] = dv_term

    @pl.when(head % GQ != 0)
    def _():
        dk_ref[0] += dk_term
        dv_ref[0] += dv_term


def unread(arrays):
    return [pl.BlockSpec(memory_space=pl.ANY)] * len(arrays)


def att_specs(rows, length):
    whole = lambda shape: pl.BlockSpec(shape, lambda h: (0, 0))
    per_q = pl.BlockSpec((1, rows, HD), lambda h: (h, 0, 0))
    per_kv = pl.BlockSpec((1, length, HD), lambda h: (h // GQ, 0, 0))
    lse = pl.BlockSpec((1, rows, 1), lambda h: (h, 0, 0))
    marks = [whole((1, length)), whole((rows, 1)), whole((1, length)), whole((rows, 1))]
    return per_q, per_kv, lse, marks


def att_cost(rows, length, dots):
    return pl.CostEstimate(
        flops=2 * dots * NHQ * rows * length * HD,
        transcendentals=NHQ * rows * length,
        bytes_accessed=4 * (NHQ * rows + NHKV * length) * HD * 2,
    )


def att_forward(q, k, v, key_doc, row_doc, key_pos, row_pos):
    rows, length = q.shape[1], k.shape[1]
    per_q, per_kv, lse, marks = att_specs(rows, length)
    return pl.pallas_call(
        att_fwd_kernel,
        name="attention_forward",
        grid=(NHQ,),
        in_specs=[per_q, per_kv, per_kv, *marks],
        out_specs=[per_q, lse],
        out_shape=[
            jax.ShapeDtypeStruct((NHQ, rows, HD), BF16),
            jax.ShapeDtypeStruct((NHQ, rows, 1), F32),
        ],
        cost_estimate=att_cost(rows, length, 2),
        compiler_params=pltpu.CompilerParams(vmem_limit_bytes=VMEM_LIMIT),
    )(q, k, v, key_doc, row_doc, key_pos, row_pos)


def att_backward(q, k, v, d_out, log_total, key_doc, row_doc, key_pos, row_pos, earlier):
    rows, length = q.shape[1], k.shape[1]
    per_q, per_kv, lse, marks = att_specs(rows, length)
    return pl.pallas_call(
        att_bwd_kernel,
        name="attention_backward",
        grid=(NHQ,),
        in_specs=[per_q, per_kv, per_kv, per_q, lse, *marks, *unread(earlier)],
        out_specs=[per_q, per_kv, per_kv],
        out_shape=[
            jax.ShapeDtypeStruct((NHQ, rows, HD), F32),
            jax.ShapeDtypeStruct((NHKV, length, HD), F32),
            jax.ShapeDtypeStruct((NHKV, length, HD), F32),
        ],
        cost_estimate=att_cost(rows, length, 5),
        compiler_params=pltpu.CompilerParams(vmem_limit_bytes=VMEM_LIMIT),
    )(q, k, v, d_out, log_total, key_doc, row_doc, key_pos, row_pos, *earlier)


def column_of(table, head):
    lanes = lax.broadcasted_iota(jnp.int32, table.shape, 1)
    return jnp.sum(jnp.where(lanes == head, table, 0.0), 1, keepdims=True)


def decay_matrix(cum_ref, cumt_ref, head):
    column = column_of(cum_ref[...], head)
    row = cumt_ref[pl.ds(head, 1), :]
    rows = column.shape[0]
    at = lax.broadcasted_iota(jnp.int32, (rows, rows), 0)
    source = lax.broadcasted_iota(jnp.int32, (rows, rows), 1)
    return column, row, jnp.exp(jnp.where(at >= source, column - row, -1e30))


def first_half_lanes(shape):
    return lax.broadcasted_iota(jnp.int32, shape, 1) < MP


def ssd_fwd_kernel(
    x_ref, b_ref, c_ref, dt_ref, cum_ref, dtt_ref, cumt_ref, y_ref, state_ref, inner
):
    pair = pl.program_id(0)
    b_in = low(b_ref[...])

    @pl.when(pair == 0)
    def _():
        inner[...] = dot_last(low(c_ref[...]), b_in)

    x_pair = x_ref[...]
    x_low = low(x_pair)
    parts, weights = [], []
    for i in range(2):
        head = 2 * pair + i
        column, row, decays = decay_matrix(cum_ref, cumt_ref, head)
        mixing = low(decays * inner[...] * dtt_ref[pl.ds(head, 1), :])
        parts.append(dot_mid(mixing, x_low))
        rows = column.shape[0]
        weights.append(jnp.exp(row[:, rows - 1 :] - column) * column_of(dt_ref[...], head))
    left = first_half_lanes(x_pair.shape)
    y_ref[...] = jnp.where(left, parts[0], parts[1])
    weighted = low(x_pair * jnp.where(left, weights[0], weights[1]))
    state_ref[...] = low(dot_first(weighted, b_in))


def ssd_bwd_kernel(
    x_ref, b_ref, c_ref, dy_ref, cum_ref, dtt_ref, cumt_ref, *rest
):
    dx_ref, db_ref, dc_ref, inner, d_inner = rest[-5:]
    pair = pl.program_id(0)
    b_in = low(b_ref[...])
    c_out = low(c_ref[...])

    @pl.when(pair == 0)
    def _():
        inner[...] = dot_last(c_out, b_in)
        d_inner[...] = jnp.zeros_like(d_inner)

    x_low = low(x_ref[...])
    dy_low = low(dy_ref[...])
    left = first_half_lanes(x_low.shape)
    parts = []
    for i in range(2):
        head = 2 * pair + i
        _, _, decays = decay_matrix(cum_ref, cumt_ref, head)
        scaled = decays * dtt_ref[pl.ds(head, 1), :]
        mixing = low(scaled * inner[...])
        parts.append(dot_first(mixing, dy_low))
        mine = left if i == 0 else jnp.logical_not(left)
        d_mixing = dot_last(jnp.where(mine, dy_low, jnp.zeros_like(dy_low)), x_low)
        d_inner[...] += d_mixing * scaled
    dx_ref[...] = jnp.where(left, parts[0], parts[1])

    @pl.when(pair == PAIRS - 1)
    def _():
        d_low = low(d_inner[...])
        dc_ref[...] = dot_mid(d_low, b_in)
        db_ref[...] = dot_first(d_low, c_out)


def ssd_join_kernel(
    x_ref, b_ref, dxl_ref, dy_ref, y_ref, state_ref, dstate_ref, dt_ref, cum_ref, cumt_ref,
    dbl_ref, dcl_ref, *rest,
):
    dx_ref, db_ref, dc_ref, row_ref, coll_ref, cols_ref, edge_ref = rest[-7:]
    pair = pl.program_id(0)
    x_pair = x_ref[...]
    left = first_half_lanes(x_pair.shape)
    rows = x_pair.shape[0]

    @pl.when(pair == 0)
    def _():
        db_ref[...] = dbl_ref[...]
        dc_ref[...] = dcl_ref[...]
        row_ref[...] = jnp.zeros_like(row_ref)
        coll_ref[...] = jnp.zeros_like(coll_ref)
        cols_ref[...] = jnp.zeros_like(cols_ref)
        edge_ref[...] = jnp.zeros_like(edge_ref)

    weights, growth, ends = [], [], []
    for i in range(2):
        head = 2 * pair + i
        column = column_of(cum_ref[...], head)
        end = cumt_ref[pl.ds(head, 1), :][:, rows - 1 :]
        weights.append(jnp.exp(end - column) * column_of(dt_ref[...], head))
        growth.append(jnp.exp(column))
        ends.append(jnp.exp(end))
    weight = jnp.where(left, weights[0], weights[1])
    grown = jnp.where(left, growth[0], growth[1])
    state = state_ref[...]
    d_state = dstate_ref[...]
    d_y = dy_ref[...]
    x_low = low(x_pair)
    weighted = low(x_pair * weight)
    through = dot_last(low(b_ref[...]), d_state)
    dx_ref[...] = dxl_ref[...] + weight * through
    db_ref[...] += dot_mid(weighted, d_state)
    dc_ref[...] += dot_mid(low(d_y * grown), state)
    row_term = f32(low(d_y)) * y_ref[...]
    local_term = f32(x_low) * dxl_ref[...]
    state_term = f32(weighted) * through
    met = f32(state) * f32(d_state)
    lanes = lax.broadcasted_iota(jnp.int32, row_ref.shape, 1)
    edge_lanes = lax.broadcasted_iota(jnp.int32, edge_ref.shape, 1)
    for i in range(2):
        mine = left if i == 0 else jnp.logical_not(left)
        here = lanes == 2 * pair + i
        for ref, term in ((row_ref, row_term), (coll_ref, local_term), (cols_ref, state_term)):
            total = jnp.sum(jnp.where(mine, term, 0.0), 1, keepdims=True)
            ref[...] = jnp.where(here, total, ref[...])
        half = met[i * MP : (i + 1) * MP]
        across = jnp.sum(jnp.sum(half, 1, keepdims=True), 0, keepdims=True) * ends[i]
        edge_ref[...] = jnp.where(edge_lanes == 2 * pair + i, across, edge_ref[...])


def ssd_cost(rows, dots, width):
    return pl.CostEstimate(
        flops=2 * dots * MH * rows * rows * PW,
        transcendentals=MH * rows * rows,
        bytes_accessed=4 * rows * MDIM * width,
    )


def ssd_specs(rows):
    pair_of = pl.BlockSpec((rows, PW), lambda p: (0, p))
    b_of = pl.BlockSpec((rows, NSTATE), lambda p: (0, PAIRS))
    c_of = pl.BlockSpec((rows, NSTATE), lambda p: (0, PAIRS + 1))
    once = pl.BlockSpec((rows, NSTATE), lambda p: (0, 0))
    tall = pl.BlockSpec((rows, MH), lambda p: (0, 0))
    wide = pl.BlockSpec((MH, rows), lambda p: (0, 0))
    state = pl.BlockSpec((PW, NSTATE), lambda p: (p, 0))
    return pair_of, b_of, c_of, once, tall, wide, state


def ssd_forward(act, dt_val, cum, dt_turned, cum_turned):
    rows = act.shape[0]
    pair_of, b_of, c_of, _, tall, wide, state = ssd_specs(rows)
    return pl.pallas_call(
        ssd_fwd_kernel,
        name="ssd_forward",
        grid=(PAIRS,),
        in_specs=[pair_of, b_of, c_of, tall, tall, wide, wide],
        out_specs=[pair_of, state],
        out_shape=[
            jax.ShapeDtypeStruct((rows, MDIM), F32),
            jax.ShapeDtypeStruct((MDIM, NSTATE), BF16),
        ],
        scratch_shapes=[pltpu.VMEM((rows, rows), F32)],
        cost_estimate=ssd_cost(rows, 1, 2),
        compiler_params=pltpu.CompilerParams(vmem_limit_bytes=VMEM_LIMIT),
    )(act, act, act, dt_val, cum, dt_turned, cum_turned)


def ssd_backward(act, d_y, cum, dt_turned, cum_turned, earlier):
    rows = act.shape[0]
    pair_of, b_of, c_of, once, tall, wide, _ = ssd_specs(rows)
    return pl.pallas_call(
        ssd_bwd_kernel,
        name="ssd_backward",
        grid=(PAIRS,),
        in_specs=[pair_of, b_of, c_of, pair_of, tall, wide, wide, *unread(earlier)],
        out_specs=[pair_of, once, once],
        out_shape=[
            jax.ShapeDtypeStruct((rows, MDIM), F32),
            jax.ShapeDtypeStruct((rows, NSTATE), F32),
            jax.ShapeDtypeStruct((rows, NSTATE), F32),
        ],
        scratch_shapes=[pltpu.VMEM((rows, rows), F32), pltpu.VMEM((rows, rows), F32)],
        cost_estimate=ssd_cost(rows, 2, 3),
        compiler_params=pltpu.CompilerParams(vmem_limit_bytes=VMEM_LIMIT),
    )(act, act, act, d_y, cum, dt_turned, cum_turned, *earlier)


def ssd_join(
    act, dx_local, d_y, y_ssd, state, d_state, dt_val, cum, cum_turned, db_local, dc_local, earlier
):
    rows = act.shape[0]
    pair_of, b_of, _, once, tall, wide, state_of = ssd_specs(rows)
    edge = pl.BlockSpec((1, MH), lambda p: (0, 0))
    return pl.pallas_call(
        ssd_join_kernel,
        name="ssd_join",
        grid=(PAIRS,),
        in_specs=[
            pair_of, b_of, pair_of, pair_of, pair_of, state_of, state_of, tall, tall, wide,
            once, once, *unread(earlier),
        ],
        out_specs=[pair_of, once, once, tall, tall, tall, edge],
        out_shape=[
            jax.ShapeDtypeStruct((rows, MDIM), F32),
            jax.ShapeDtypeStruct((rows, NSTATE), F32),
            jax.ShapeDtypeStruct((rows, NSTATE), F32),
            jax.ShapeDtypeStruct((rows, MH), F32),
            jax.ShapeDtypeStruct((rows, MH), F32),
            jax.ShapeDtypeStruct((rows, MH), F32),
            jax.ShapeDtypeStruct((1, MH), F32),
        ],
        cost_estimate=pl.CostEstimate(
            flops=6 * rows * MDIM * NSTATE,
            transcendentals=3 * rows * MH,
            bytes_accessed=4 * rows * MDIM * 5,
        ),
        compiler_params=pltpu.CompilerParams(vmem_limit_bytes=VMEM_LIMIT),
    )(
        act, act, dx_local, d_y, y_ssd, state, d_state, dt_val, cum, cum_turned, db_local, dc_local,
        *earlier,
    )


STEPS = 4


def square_of(ref):
    block = ref[...]
    return block.reshape(block.shape[0] * block.shape[1], block.shape[2])


def call_ffn(kernel, name, in_specs, out_specs, out_shape, flops, operands, scratch=()):
    return pl.pallas_call(
        kernel,
        name=name,
        grid=(STEPS,),
        in_specs=in_specs,
        out_specs=out_specs,
        out_shape=out_shape,
        scratch_shapes=list(scratch),
        cost_estimate=pl.CostEstimate(flops=flops, transcendentals=0, bytes_accessed=flops // 256),
        compiler_params=pltpu.CompilerParams(vmem_limit_bytes=VMEM_LIMIT),
    )(*operands)


def whole_of(shape):
    return pl.BlockSpec(shape, lambda k: (0,) * len(shape))


def column_block(rows, width):
    return pl.BlockSpec((rows, width), lambda k: (0, k))


def devices_block(stack, part):
    count, tall, _ = stack.shape
    return pl.BlockSpec((count // STEPS, tall // 4, D), lambda k: (k, part, 0))


def middle_kernel(hidden_ref, joined_ref, w_ref, gain_ref, middle_ref, ff_ref, scale_ref):
    step = pl.program_id(0)
    term = dot_mid(joined_ref[...], square_of(w_ref))

    @pl.when(step == 0)
    def _():
        middle_ref[...] = f32(hidden_ref[...]) + term

    @pl.when(step != 0)
    def _():
        middle_ref[...] += term

    @pl.when(step == STEPS - 1)
    def _():
        middle = middle_ref[...]
        scale = lax.rsqrt(jnp.mean(middle * middle, -1, keepdims=True) + EPS)
        scale_ref[...] = scale
        ff_ref[...] = low(middle * scale * gain_ref[...])


def ffn_middle(hidden, joined, stack, gain):
    rows, width = joined.shape
    return call_ffn(
        middle_kernel,
        "middle",
        [
            whole_of((rows, D)),
            column_block(rows, width // STEPS),
            devices_block(stack, 2),
            whole_of((1, D)),
        ],
        [whole_of((rows, D)), whole_of((rows, D)), whole_of((rows, 1))],
        [
            jax.ShapeDtypeStruct((rows, D), F32),
            jax.ShapeDtypeStruct((rows, D), BF16),
            jax.ShapeDtypeStruct((rows, 1), F32),
        ],
        2 * rows * width * D,
        (hidden, joined, stack, gain),
    )


def gate_kernel(ff_ref, gate_w_ref, up_w_ref, gate_ref, up_ref, act_ref):
    ff = ff_ref[...]
    gate = dot_mid(ff, square_of(gate_w_ref))
    up = dot_mid(ff, square_of(up_w_ref))
    gate_ref[...] = gate
    up_ref[...] = up
    act_ref[...] = low(gate * jax.nn.sigmoid(gate) * up)


def ffn_gate(ff, stack):
    rows = ff.shape[0]
    count, tall, _ = stack.shape
    quarter = lambda first: pl.BlockSpec(
        (count, tall // 8, D // 2), lambda k: (0, first + k // 2, k % 2)
    )
    out = column_block(rows, FF // STEPS)
    return call_ffn(
        gate_kernel,
        "gate_up",
        [whole_of((rows, D)), quarter(0), quarter(2)],
        [out, out, out],
        [
            jax.ShapeDtypeStruct((rows, FF), F32),
            jax.ShapeDtypeStruct((rows, FF), F32),
            jax.ShapeDtypeStruct((rows, FF), BF16),
        ],
        4 * rows * FF * D,
        (ff, stack, stack),
    )


def output_kernel(middle_ref, act_ref, w_ref, *rest):
    out_ref, total = rest[-2:]
    step = pl.program_id(0)
    term = dot_mid(act_ref[...], square_of(w_ref))

    @pl.when(step == 0)
    def _():
        total[...] = middle_ref[...] + term

    @pl.when(step != 0)
    def _():
        total[...] += term

    @pl.when(step == STEPS - 1)
    def _():
        out_ref[...] = low(total[...])


def ffn_output(middle, act, stack, earlier):
    rows, width = act.shape
    return call_ffn(
        output_kernel,
        "layer_output",
        [
            whole_of((rows, D)),
            column_block(rows, width // STEPS),
            devices_block(stack, 3),
            *unread(earlier),
        ],
        whole_of((rows, D)),
        jax.ShapeDtypeStruct((rows, D), BF16),
        2 * rows * width * D,
        (middle, act, stack, *earlier),
        [pltpu.VMEM((rows, D), F32)],
    )


def d_gate_kernel(cot_ref, w_ref, gate_ref, up_ref, *rest):
    d_ref = rest[-1]
    step = pl.program_id(0)
    width = gate_ref.shape[1]
    d_act = dot_last(cot_ref[...], square_of(w_ref))
    gate = gate_ref[...]
    sigma = jax.nn.sigmoid(gate)
    start = pl.multiple_of(step * width, 128)
    d_ref[:, pl.ds(start, width)] = low(d_act * up_ref[...] * silu_slope(gate, sigma))
    d_ref[:, pl.ds(start + FF, width)] = low(d_act * (gate * sigma))


def ffn_d_gate(cot, stack, gate, up, earlier):
    rows = cot.shape[0]
    block = column_block(rows, FF // STEPS)
    return call_ffn(
        d_gate_kernel,
        "d_gate_up",
        [whole_of((rows, D)), devices_block(stack, 3), block, block, *unread(earlier)],
        whole_of((rows, 2 * FF)),
        jax.ShapeDtypeStruct((rows, 2 * FF), BF16),
        2 * rows * FF * D,
        (cot, stack, gate, up, *earlier),
    )


def d_middle_kernel(d_gu_ref, w_ref, middle_ref, scale_ref, gain_ref, cot_ref, *rest):
    d_ref, low_ref, gain_grad_ref = rest[-3:]
    step = pl.program_id(0)
    term = dot_last(d_gu_ref[...], square_of(w_ref))

    @pl.when(step == 0)
    def _():
        d_ref[...] = term

    @pl.when(step != 0)
    def _():
        d_ref[...] += term

    @pl.when(step == STEPS - 1)
    def _():
        d_normed = d_ref[...]
        scale = scale_ref[...]
        unit = middle_ref[...] * scale
        gain_grad_ref[...] = jnp.sum(d_normed * unit, 0, keepdims=True)
        d_unit = d_normed * gain_ref[...]
        inner = jnp.mean(d_unit * unit, -1, keepdims=True)
        d_middle = f32(cot_ref[...]) + scale * (d_unit - unit * inner)
        d_ref[...] = d_middle
        low_ref[...] = low(d_middle)


def ffn_d_middle(d_gu, stack, middle, scale, gain, cot, earlier):
    rows = d_gu.shape[0]
    count, tall, _ = stack.shape
    whole = whole_of((rows, D))
    return call_ffn(
        d_middle_kernel,
        "d_middle",
        [
            column_block(rows, D),
            pl.BlockSpec((count, tall // 8, D), lambda k: (0, k, 0)),
            whole,
            whole_of((rows, 1)),
            whole_of((1, D)),
            whole,
            *unread(earlier),
        ],
        [whole, whole, whole_of((1, D))],
        [
            jax.ShapeDtypeStruct((rows, D), F32),
            jax.ShapeDtypeStruct((rows, D), BF16),
            jax.ShapeDtypeStruct((1, D), F32),
        ],
        4 * rows * FF * D,
        (d_gu, stack, middle, scale, gain, cot, *earlier),
    )


def d_joined_kernel(d_ref, w_ref, out_ref):
    out_ref[...] = low(dot_last(d_ref[...], square_of(w_ref)))


def mixer_d_joined(d_middle, stack):
    rows = d_middle.shape[0]
    width = 2 * D
    return call_ffn(
        d_joined_kernel,
        "d_joined",
        [whole_of((rows, D)), devices_block(stack, 2)],
        column_block(rows, width // STEPS),
        jax.ShapeDtypeStruct((rows, width), BF16),
        2 * rows * width * D,
        (d_middle, stack),
    )


def flipped(value, bit):
    count = lax.axis_size("fsdp")
    return lax.ppermute(value, "fsdp", [(i, i ^ bit) for i in range(count)])


def squares():
    return lax.axis_size("fsdp") == 8


def gather_rows(shard):
    return lax.all_gather(shard, "fsdp", axis=0, tiled=True)


def device_columns(left, flips, depth, offset):
    count = lax.axis_size("fsdp")
    stride = left.shape[1] // count
    me = lax.axis_index("fsdp")
    return jnp.concatenate(
        [
            lax.dynamic_slice_in_dim(left, (me ^ flip) * stride + offset, depth, 1)
            for flip in flips
        ],
        1,
    )


def products_kernel(left_ref, right_ref, *rest):
    out_ref = rest[-1]
    term = dot_first(left_ref[0], right_ref[...]).reshape(out_ref.shape)
    if len(rest) > 1:
        term = term + f32(rest[0][...])
    out_ref[...] = low(term)


def products(lefts, right, group, came=()):
    rows, columns = right.shape
    depth, step = group.depth, group.step
    out = pl.BlockSpec((4, depth, step), lambda k: (0, 0, k))
    return pl.pallas_call(
        products_kernel,
        name="gradient_rows",
        grid=(columns // step,),
        in_specs=[
            pl.BlockSpec((1, rows, 4 * depth), lambda k: (group.left_of(k), 0, 0)),
            pl.BlockSpec((rows, step), lambda k: (0, k)),
            *([out] * len(came)),
        ],
        out_specs=out,
        out_shape=jax.ShapeDtypeStruct((4, depth, columns), BF16),
        cost_estimate=pl.CostEstimate(
            flops=8 * rows * depth * columns,
            transcendentals=0,
            bytes_accessed=8 * depth * columns * (1 + len(came)),
        ),
        compiler_params=pltpu.CompilerParams(vmem_limit_bytes=VMEM_LIMIT),
    )(lefts, right, *came)


class Group:
    def __init__(self, lefts, counts, depth, step, left_of):
        self.counts, self.depth, self.step, self.left_of = counts, depth, step, left_of
        self.lefts = lefts
        if squares():
            self.theirs, self.mine = [
                jnp.stack([device_columns(left, flips, depth, at) for left, at in lefts])
                for flips in ((1, 3, 5, 7), (0, 2, 4, 6))
            ]


def scatter_open(group, right):
    if squares():
        return products(group.theirs, right, group)
    count = lax.axis_size("fsdp")
    whole, first = [], 0
    for (left, at), columns in zip(group.lefts, group.counts):
        rows = left.reshape(left.shape[0], count, -1)[:, :, at : at + group.depth]
        part = right[:, first : first + columns]
        whole.append(low(dot_first(rows.reshape(left.shape[0], -1), part)))
        first += columns
    return lax.psum_scatter(
        jnp.concatenate(whole, 1), "fsdp", scatter_dimension=0, tiled=True
    )


def scatter_swap(group, right, theirs):
    if not squares():
        return theirs
    return products(group.mine, right, group, [flipped(theirs, 1)])


def scatter_first(ours):
    if not squares():
        return ours, ours
    half = ours.shape[1] // 2
    for_y = flipped(ours[3, :half], 2)
    for_x = flipped(ours[3, half:], 4)
    to_x = jnp.concatenate([ours[1, :half], low(f32(ours[1, half:]) + f32(for_x))], 0)
    to_y = jnp.concatenate([low(f32(ours[2, :half]) + f32(for_y)), ours[2, half:]], 0)
    return to_x, to_y


def scatter_last(ours, to_x, to_y):
    if not squares():
        return ours
    return low(f32(ours[0]) + f32(flipped(to_x, 2)) + f32(flipped(to_y, 4)))


def grid_total(value):
    if not squares() or lax.axis_size("ctx") != 4:
        return lax.psum(value, ("ctx", "fsdp"))
    for bit in (1, 2, 4):
        value = value + flipped(value, bit)
    for bit in (1, 2):
        value = value + ctx_flipped(value, bit)
    return value


def ctx_flipped(value, bit):
    return lax.ppermute(value, "ctx", [(i, i ^ bit) for i in range(lax.axis_size("ctx"))])


def ctx_total(part, earlier=()):
    if lax.axis_size("ctx") != 4:
        return f32(lax.psum(part, "ctx"))
    me = lax.axis_index("ctx")
    value = part
    for bit in (1, 2):
        size = value.shape[0] // 2
        upper = (me // bit) % 2
        mine = lax.dynamic_slice_in_dim(value, upper * size, size, 0)
        theirs = lax.dynamic_slice_in_dim(value, (1 - upper) * size, size, 0)
        value = low(f32(mine) + f32(ctx_flipped(theirs, bit)))
    value = after(value, earlier)
    for bit in (2, 1):
        upper = (me // bit) % 2
        other = ctx_flipped(value, bit)
        value = jnp.concatenate(
            [jnp.where(upper == 0, value, other), jnp.where(upper == 0, other, value)], 0
        )
    return f32(value)


def entering(own, decay, direction):
    count = lax.axis_size("ctx")
    coarse = low(decay)
    fine = low(decay - f32(coarse))
    line = jnp.concatenate([coarse, fine, jnp.zeros((NSTATE - 2 * MH,), BF16)])
    packed = jnp.concatenate([own, jnp.broadcast_to(line[None], (16, NSTATE))], 0)
    total = jnp.zeros(own.shape, F32)
    carried = jnp.ones(decay.shape, F32)
    for distance in range(1, count):
        came = shifted(packed, "ctx", direction * distance)
        total = total + f32(came[:MDIM]) * jnp.repeat(carried, MP)[:, None]
        line = f32(came[MDIM])
        carried = carried * (line[:MH] + line[MH : 2 * MH])
    return total


def after(value, earlier):
    return lax.optimization_barrier((value, earlier))[0]


def silu_slope(value, sigma):
    return sigma * (1.0 + value * (1.0 - sigma))


def body(
    hidden,
    cotangent,
    doc_ids,
    mixer_in_weight,
    mixer_out_weight,
    feedforward_in_weight,
    feedforward_out_weight,
    gain_in,
    gain_ff,
    gain_mix,
    conv_weight,
    conv_bias,
    dt_bias,
    a_log,
    d_skip,
):
    rows = hidden.shape[1]
    shards = lax.axis_size("fsdp")

    small = [gain_in, gain_ff, gain_mix, conv_weight.T.reshape(-1), conv_bias]
    sizes = [piece.shape[0] for piece in small]
    depth = mixer_in_weight.shape[0]
    width_cd = NIN - QKV - MDIM
    lines = -(-sum(sizes) // depth)
    line = jnp.concatenate(small + [jnp.zeros((lines * depth - sum(sizes),), BF16)])
    full_in = gather_rows(
        jnp.concatenate([mixer_in_weight, line.reshape(lines, depth).T], 1)
    )
    full_qkv = full_in[:, :QKV]
    full_z = full_in[:, QKV : QKV + MDIM]
    full_cd = full_in[:, QKV + MDIM : NIN]

    small_all = f32(full_in[:, NIN:]).T.reshape(lines, shards, depth)
    small_all = small_all.transpose(1, 0, 2).reshape(shards, lines * depth)
    cuts = [sum(sizes[:i]) for i in range(len(sizes) + 1)]
    gin, gff, gmix, convw, convb = [
        small_all[:, cuts[i] : cuts[i + 1]] for i in range(len(sizes))
    ]
    gin, gff, gmix, convb = [piece.reshape(-1) for piece in (gin, gff, gmix, convb)]
    convw = convw.reshape(shards, CONVK, -1).transpose(1, 0, 2).reshape(CONVK, CONVC)

    quarters = [feedforward_in_weight[:, i * D : (i + 1) * D] for i in range(4)]
    stack = lax.all_gather(
        jnp.concatenate([*quarters, mixer_out_weight, feedforward_out_weight], 0), "fsdp", axis=0
    )

    hidden32 = f32(hidden[0])
    scale_in = lax.rsqrt(jnp.mean(hidden32 * hidden32, -1, keepdims=True) + EPS)
    normed_b = low(hidden32 * scale_in * gin)

    proj_cd = dot_mid(normed_b, full_cd)
    conv_in = proj_cd[:, :CONVC]
    dt_raw = proj_cd[:, CONVC:]
    rim = shifted(conv_in[rows - (CONVK - 1) :], "ctx", 1)
    extended = jnp.concatenate([rim, conv_in], 0)
    u = convb
    for tap in range(CONVK):
        u = u + convw[tap] * extended[tap : tap + rows]
    u_sigma = jax.nn.sigmoid(u)
    act = u * u_sigma
    dt_arg = dt_raw + dt_bias
    dt_val = jax.nn.softplus(dt_arg)
    rate = -jnp.exp(a_log)
    log_decay = rate * dt_val
    ones = (jnp.arange(rows)[:, None] >= jnp.arange(rows)[None, :]).astype(F32)
    cum = lax.dot_general(ones, log_decay, (((1,), (0,)), ((), ())), precision=FULL_PRECISION)
    cum_turned = cum.T
    dt_turned = dt_val.T
    y_local, own_state = ssd_forward(act, dt_val, cum, dt_turned, cum_turned)
    own_decay = jnp.exp(cum[-1])

    proj_qkv = dot_mid(normed_b, full_qkv)
    positions = lax.axis_index("ctx") * rows + jnp.arange(rows)
    cos_tab, sin_tab = rope_tables(positions)
    q_heads = low(rotate_heads(heads_first(proj_qkv[:, :ATTW]), cos_tab, sin_tab))
    k_heads = low(rotate_heads(heads_first(proj_qkv[:, ATTW : ATTW + KVW]), cos_tab, sin_tab))
    v_heads = low(heads_first(proj_qkv[:, ATTW + KVW :]))
    doc_here = low(doc_ids[0])
    doc_line = jnp.concatenate([doc_here, jnp.zeros((2 * KVW - rows,), BF16)])
    own_kv = jnp.concatenate(
        [
            jnp.concatenate([heads_flat(k_heads), heads_flat(v_heads)], 1),
            jnp.broadcast_to(doc_line[None], (16, 2 * KVW)),
        ],
        0,
    )
    blocks = lax.axis_size("ctx")
    me = lax.axis_index("ctx")
    came = [own_kv] + [shifted(own_kv, "ctx", distance) for distance in range(1, blocks)]
    kv_all = jnp.concatenate([block[:rows] for block in came], 0)
    k_all = heads_first(kv_all[:, :KVW])
    v_all = heads_first(kv_all[:, KVW:])
    key_doc = jnp.concatenate([block[rows, :rows] for block in came])[None, :].astype(jnp.int32)
    row_doc = doc_ids[0][:, None]
    row_pos = positions.astype(jnp.int32)[:, None]
    key_pos = jnp.concatenate(
        [
            jnp.where(me >= distance, positions - distance * rows, blocks * rows)
            for distance in range(blocks)
        ]
    )[None, :]
    attended, log_total = att_forward(q_heads, k_all, v_all, key_doc, row_doc, key_pos, row_pos)

    state_in = low(entering(own_state, own_decay, 1))
    spread = (jnp.arange(MH)[:, None] == (jnp.arange(MDIM) // MP)[None, :]).astype(F32)
    grown = lax.dot_general(
        jnp.exp(cum), spread, (((1,), (0,)), ((), ())), precision=FULL_PRECISION
    )
    x_flat = act[:, :MDIM]
    c_low = low(act[:, MDIM + NSTATE :])
    y_ssd = y_local + grown * dot_last(c_low, state_in)
    z_gate = dot_mid(normed_b, full_z)
    skip = jnp.repeat(d_skip, MP)
    y_full = y_ssd + skip * x_flat
    z_sigma = jax.nn.sigmoid(z_gate)
    z_act = z_gate * z_sigma
    gated = y_full * z_act
    scale_mix = lax.rsqrt(jnp.mean(gated * gated, -1, keepdims=True) + EPS)
    joined_b = jnp.concatenate(
        [heads_flat(attended), low(gated * scale_mix * gmix)], 1
    )

    cot_b = cotangent[0]
    middle, ff_b, scale_ff = ffn_middle(hidden[0], joined_b, stack, gff[None])
    gate_val, up_val, act_b = ffn_gate(ff_b, stack)

    grad_fo = low(dot_first(act_b, cot_b))
    part_fo = lax.psum_scatter(grad_fo, "fsdp", scatter_dimension=0, tiled=True)
    d_gu = ffn_d_gate(cot_b, stack, gate_val, up_val, [grad_fo])
    grad_fi = low(dot_first(ff_b, d_gu))
    part_fi = lax.psum_scatter(grad_fi, "fsdp", scatter_dimension=0, tiled=True)
    d_middle, d_middle_b, dg_ff = ffn_d_middle(
        d_gu, stack, middle, scale_ff, gff[None], cot_b, [grad_fi]
    )
    dg_ff = dg_ff[0]
    d_joined = mixer_d_joined(d_middle_b, stack)
    d_mamba = f32(d_joined[:, ATTW:])
    unit_mix = gated * scale_mix
    dg_mix = jnp.sum(d_mamba * unit_mix, 0)
    d_unit_mix = d_mamba * gmix
    d_gated = scale_mix * (
        d_unit_mix - unit_mix * jnp.mean(d_unit_mix * unit_mix, -1, keepdims=True)
    )
    d_y = d_gated * z_act
    d_z = low(d_gated * y_full * silu_slope(z_gate, z_sigma))
    dd_skip = jnp.sum(jnp.sum(d_y * x_flat, 0).reshape(MH, MP), 1)
    local_grad = low(dot_first(low(d_y * grown), c_low))

    group_m = Group(
        [(joined_b, 0), (joined_b, depth), (normed_b, 0)],
        [D, D, MDIM],
        depth,
        D // 2,
        lambda k: jnp.minimum(k // 2, 2),
    )
    right_m = jnp.concatenate([d_middle_b, d_middle_b, d_z], 1)
    theirs_m = scatter_open(group_m, right_m)

    dx_local, db_local, dc_local = ssd_backward(
        act, d_y, cum, dt_turned, cum_turned, [local_grad]
    )
    d_state = low(entering(local_grad, own_decay, -1))
    do_heads = heads_first(d_joined[:, :ATTW])
    d_q, d_k, d_v = att_backward(
        q_heads, k_all, v_all, do_heads, log_total, key_doc, row_doc, key_pos, row_pos,
        [dx_local],
    )
    d_kv = jnp.concatenate([heads_flat(d_k), heads_flat(d_v)], 1)
    terms = low(d_kv[rows:])
    terms = after(terms, d_state)
    dx_ssd, d_b, d_c, row_term, col_local, col_state, edge = ssd_join(
        act, dx_local, d_y, y_ssd, state_in, d_state, dt_val, cum, cum_turned, db_local, dc_local,
        [theirs_m, part_fo, terms],
    )
    received = [
        shifted(terms[(distance - 1) * rows : distance * rows], "ctx", -distance)
        for distance in range(1, blocks)
    ]
    received, dx_ssd = lax.optimization_barrier((received, dx_ssd))
    dkv = d_kv[:rows] + sum(f32(term) for term in received)
    d_q = rotate_heads(d_q, cos_tab, -sin_tab)
    d_k = rotate_heads(heads_first(dkv[:, :KVW]), cos_tab, -sin_tab)
    d_qkv = jnp.concatenate([low(heads_flat(d_q)), low(heads_flat(d_k)), low(dkv[:, KVW:])], 1)
    col_term = col_local + col_state
    d_cum = row_term - col_term
    d_end = jnp.sum(col_state, 0) + edge[0]
    d_decay = (
        lax.dot_general(ones, d_cum, (((0,), (0,)), ((), ())), precision=FULL_PRECISION) + d_end
    )
    d_alog = jnp.sum(d_decay * log_decay, 0)
    dt_sigma = jax.nn.sigmoid(dt_arg)
    ratio = jnp.where(dt_arg < -30.0, 1.0, dt_sigma / jnp.where(dt_arg < -30.0, 1.0, dt_val))
    d_dtraw = col_term * ratio + d_decay * rate * dt_sigma
    d_dtbias = jnp.sum(d_dtraw, 0)

    d_act_conv = jnp.concatenate([dx_ssd + skip * d_y, d_b, d_c], 1)
    d_u = d_act_conv * silu_slope(u, u_sigma)
    d_convb = jnp.sum(d_u, 0)
    d_convw = jnp.stack(
        [jnp.sum(d_u * extended[tap : tap + rows], 0) for tap in range(CONVK)]
    )
    d_u_ext = jnp.concatenate([d_u, shifted(d_u[: CONVK - 1], "ctx", -1)], 0)
    d_conv_in = sum(
        convw[tap] * d_u_ext[CONVK - 1 - tap : CONVK - 1 - tap + rows] for tap in range(CONVK)
    )
    d_cd = jnp.concatenate([low(d_conv_in), low(d_dtraw)], 1)
    d_cd = after(d_cd, part_fi)
    lone = jnp.zeros((rows, -(QKV + width_cd) % 384), BF16)
    right_c = jnp.concatenate([d_qkv, d_cd, lone], 1)
    group_c = Group([(normed_b, 0)], [right_c.shape[1]], depth, 384, lambda k: 0)
    theirs_c = scatter_open(group_c, right_c)
    ours_m = scatter_swap(group_m, right_m, after(theirs_m, theirs_c))
    to_x_m, to_y_m = scatter_first(ours_m)
    ours_c = scatter_swap(group_c, right_c, theirs_c)
    ours_c = after(ours_c, (to_x_m, to_y_m))
    to_x_c, to_y_c = scatter_first(ours_c)
    part_m = scatter_last(ours_m, to_x_m, to_y_m)
    part_c = scatter_last(ours_c, to_x_c, to_y_c)

    d_normed = dot_last(d_cd, full_cd) + dot_last(d_qkv, full_qkv) + dot_last(d_z, full_z)
    unit_in = hidden32 * scale_in
    dg_in = jnp.sum(d_normed * unit_in, 0)
    d_unit_in = d_normed * gin
    d_hidden = d_middle + scale_in * (
        d_unit_in - unit_in * jnp.mean(d_unit_in * unit_in, -1, keepdims=True)
    )

    result = ffn_output(middle, act_b, stack, [part_c])
    tot_f = lax.psum((part_fo, part_fi), "ctx")
    tot_f, parts = lax.optimization_barrier((tot_f, (part_m, part_c)))
    tot_m, tot_c = [f32(total) for total in lax.psum(parts, "ctx")]
    tot_fo, tot_fi = [f32(total) for total in tot_f]
    tot_mo = jnp.concatenate([tot_m[:, :D], tot_m[:, D : 2 * D]], 0)
    small_grads = jnp.concatenate(
        [dg_in, dg_ff, dg_mix, d_convw.reshape(-1), d_convb, d_dtbias, d_alog, dd_skip]
    )
    small_total = grid_total(small_grads)
    mine = lax.axis_index("fsdp")
    place = 0

    def own_part(width, count=1):
        nonlocal place
        block = small_total[place : place + width * count].reshape(count, width)
        place += width * count
        return lax.dynamic_slice_in_dim(block, mine * (width // shards), width // shards, 1)

    tg_in = own_part(D)[0]
    tg_ff = own_part(D)[0]
    tg_mix = own_part(MDIM)[0]
    t_convw = own_part(CONVC, CONVK).T
    t_convb = own_part(CONVC)[0]
    heads = small_total[place:].reshape(3, MH)
    return (
        result[None],
        d_hidden[None],
        jnp.concatenate([tot_c[:, :QKV], tot_m[:, 2 * D :], tot_c[:, QKV : QKV + width_cd]], 1),
        tot_mo,
        tot_fi,
        tot_fo,
        tg_in,
        tg_ff,
        tg_mix,
        t_convw,
        t_convb,
        heads[0],
        heads[1],
        heads[2],
    )


def solution(mesh):
    return jax.shard_map(
        body,
        mesh=mesh,
        in_specs=(
            P("fsdp", "ctx", None),
            P("fsdp", "ctx", None),
            P("fsdp", "ctx"),
            P("fsdp", None),
            P("fsdp", None),
            P("fsdp", None),
            P("fsdp", None),
            P("fsdp"),
            P("fsdp"),
            P("fsdp"),
            P("fsdp", None),
            P("fsdp"),
            P(),
            P(),
            P(),
        ),
        out_specs=(
            P("fsdp", "ctx", None),
            P("fsdp", "ctx", None),
            P("fsdp", None),
            P("fsdp", None),
            P("fsdp", None),
            P("fsdp", None),
            P("fsdp"),
            P("fsdp"),
            P("fsdp"),
            P("fsdp", None),
            P("fsdp"),
            P(),
            P(),
            P(),
        ),
        check_vma=False,
    )
```
